32 devices in a mesh: fsdp: 8 (over z, x), rep: 4 (over y, core).
Axes of the slice: x: 2, y: 2, z: 4, core: 2. Of those that a mesh axis runs over, the one named last changes fastest.
Arguments:
- tokens: bfloat16 [16384, 768], P(('fsdp', 'rep')), may hold values from -6 to 6
- attn_gain: bfloat16 [768], P(('fsdp', 'rep')), may hold values from 0.5 to 1.5
- qkv_weight: bfloat16 [768, 2304], P(('fsdp', 'rep')), may hold values from -0.21875 to 0.21875
- out_weight: bfloat16 [768, 768], P(('fsdp', 'rep')), may hold values from -1.25 to 1.25
- ffn_gain: bfloat16 [768], P(('fsdp', 'rep')), may hold values from 0.5 to 1.5
- router_weight: bfloat16 [768, 8], P(('fsdp', 'rep')), may hold values from -0.15625 to 0.15625
- expert_in: bfloat16 [8, 768, 3072], P('fsdp', 'rep'), may hold values from -0.21875 to 0.21875
- expert_out: bfloat16 [8, 3072, 768], P('fsdp', 'rep'), may hold values from -0.15625 to 0.15625
- bias_table: float32 [12, 32], replicated, may hold values from -4 to 4
- seq_lengths: int32 [32, 4], P(('fsdp', 'rep')), may hold values from 1 to 384, 512 in all within a row
- bucket_map: int32 [384], replicated, may hold values from 0 to 31
- expert_ids: int32 [16384, 2], P(('fsdp', 'rep')), may hold values from 0 to 7, all different within a row; in each aligned block of 512 rows (0 to 511, 512 to 1023, ...) at most 256 rows name the same one
- cotangent: bfloat16 [16384, 768], P(('fsdp', 'rep')), may hold values from -6 to 6
Outputs:
- output: bfloat16 [16384, 768], P(('fsdp', 'rep'))
- token_grad: float32 [16384, 768], P(('fsdp', 'rep'))
- attn_gain_grad: float32 [768], P(('fsdp', 'rep'))
- qkv_grad: float32 [768, 2304], P(('fsdp', 'rep'))
- out_grad: float32 [768, 768], P(('fsdp', 'rep'))
- ffn_gain_grad: float32 [768], P(('fsdp', 'rep'))
- router_grad: float32 [768, 8], P(('fsdp', 'rep'))
- expert_in_grad: float32 [8, 768, 3072], P('fsdp', 'rep')
- expert_out_grad: float32 [8, 3072, 768], P('fsdp', 'rep')
- bias_grad: float32 [12, 32], replicated
The draws below stay inside these ranges and needn't reach their ends.
Inputs may be any that keep to these rules, and one draw needn't show every extreme that they name: `seq_lengths`: each row lists the 4 sequences of one device in order and sums to 512; each row's longest is exactly 384. `expert_ids`: A token's two experts differ. In the rows of one device no expert is named by more than 256 rows, and in every draw some expert is named by exactly 256 rows of some device.
All inputs are finite; a program needn't handle non-finite values.
Results may differ from the reference program's by a relative error of at most 0.013.
Values may be sent and summed in bfloat16 or wider, within the bound.
No kernel may reach another device: no remote copies, remote signals or barrier semaphores. Data moves between devices by JAX's collectives and lax.ppermute only.
A program may use at most 192 MiB of HBM per device.

```python
import math
import jax
import jax.numpy as jnp
import numpy as np
from jax import lax

D = 768
HEADS = 12
HEAD_DIM = 64
FF = 3072
BUCKETS = 32
TOK_DEV = 512
SEQ_DEV = 4
MAXLEN = 384
EXPERTS = 8
CAP = 256
TOKENS = 16384
N_FSDP = 8
N_REP = 4
DEVICES = 32


def with_ends(result, own_key, smallest, top_value):
    longest = result.shape.index(max(result.shape))
    spots = []
    for shift in (0, 1):
        where = [jax.random.randint(jax.random.fold_in(own_key, axis), (), 0, length) for axis, length in enumerate(result.shape)]
        where[longest] = (where[longest] + shift) % result.shape[longest]
        spots.append(tuple(where))
    return result.at[spots[0]].set(smallest).at[spots[1]].set(top_value)


def shard_levels(stream_key, extent, cuts, smallest, high):
    factor_of, own = 1.0, jax.random.fold_in(stream_key, 6)
    for dim, shards_of in cuts:
        steps = jnp.exp(jax.random.uniform(jax.random.fold_in(own, dim), (shards_of,), jnp.float32, smallest / len(cuts), high / len(cuts)))
        factor_of = factor_of * jnp.repeat(steps, extent[dim] // shards_of).reshape([-1 if axis == dim else 1 for axis in range(len(extent))])
    return factor_of


def length_profile(count, total, reach, slope):
    loads = [(1 << 20) // math.isqrt(rank ** slope) + 1 for rank in range(2, count + 1)]
    rest, given = total - reach - (count - 1), [1] * (count - 1)
    while rest > 0:
        movable = [i for i in range(count - 1) if given[i] < reach]
        whole, left = sum([loads[i] for i in movable]), rest
        for i in movable:
            extra = min(reach - given[i], max(1, left * loads[i] // whole), rest)
            given[i] = given[i] + extra
            rest = rest - extra
    return np.array([reach] + given)


def uneven(key, number_of, total, limit, skew):
    if number_of == 2:
        one = jax.random.randint(key, (), max(1, total - limit), min(limit, total - 1) + 1)
        return jnp.stack([one, total - one])
    sizes = jnp.asarray(length_profile(number_of, total, limit, skew), jnp.int32)
    pairs = (number_of - 1) // 2
    donor, receiver = sizes[1:1 + 2 * pairs:2], sizes[2:2 + 2 * pairs:2]
    slack = jnp.minimum(donor - 1, limit - receiver)
    passed = jax.random.randint(jax.random.fold_in(key, 1), (pairs,), 0, 1 << 20) % (slack + 1)
    sizes = sizes.at[1:1 + 2 * pairs:2].set(donor - passed).at[2:2 + 2 * pairs:2].set(receiver + passed)
    return sizes[jax.random.permutation(jax.random.fold_in(key, 2), number_of)]


def assign_block(own_key, own, number, rows, count, top, limit, skew):
    sequence = jax.random.permutation(own_key, count)
    heavy_load, common = load_shares(count, rows * top, limit, skew, True), load_shares(count, rows * top, limit, skew, False)
    places = jnp.arange(count)

    def named(sizes, offset_by):
        used = int((sizes > 0).sum())
        fixed = max(1, used // 4)
        shifted = fixed + (places - fixed + offset_by * (used - fixed)) % max(1, count - fixed)
        return jnp.zeros((count,), jnp.int32).at[sequence[jnp.where(places < fixed, places, shifted)]].set(jnp.asarray(sizes, jnp.int32))

    sizes = jnp.where(number % 4 == 0, named(heavy_load, number // 4), named(common, number - number // 4 - 1))
    mixed = jax.random.permutation(jax.random.fold_in(own, 3), count)
    giver, receiver = mixed[0:count // 2 * 2:2], mixed[1:count // 2 * 2:2]
    margin = jnp.minimum(sizes[giver] - 1, limit - sizes[receiver]) // 2
    margin = jnp.where((giver == sequence[0]) | (receiver == sequence[0]) | (sizes[receiver] == 0), 0, jnp.maximum(margin, 0))
    shifted = jax.random.randint(jax.random.fold_in(own, 4), (count // 2,), 0, 1 << 20) % (margin + 1)
    sizes = sizes.at[giver].add(-shifted).at[receiver].add(shifted)
    members = jnp.searchsorted(jnp.cumsum(sizes), jnp.arange(rows * top), side="right").astype(jnp.int32)
    grid = members.reshape(top, rows).T
    grid = grid[jax.random.permutation(jax.random.fold_in(own, 1), rows)]
    offset_by = jax.random.randint(jax.random.fold_in(own, 2), (rows, 1), 0, top)
    return jnp.take_along_axis(grid, (jnp.arange(top)[None, :] + offset_by) % top, axis=1)


def load_shares(count, total, bound, lean, full):
    weights = [(1 << 20) // math.isqrt(grade ** lean) + 1 for grade in range(1, count + 1)]
    largest = bound if full else min(bound, max(-(-total // count), total * weights[0] // sum(weights)))
    least = 1 if total - largest >= count - 1 else 0
    counts, rest = [largest] + [least] * (count - 1), total - largest - least * (count - 1)
    while rest > 0:
        candidates = [i for i in range(1, count) if counts[i] < largest] or [i for i in range(1, count) if counts[i] < bound]
        pool, left = sum([weights[i] for i in candidates]), rest
        for i in candidates:
            more = min(bound - counts[i], max(1, left * weights[i] // pool), rest)
            counts[i] = counts[i] + more
            rest = rest - more
    return np.array(counts)


def centred(rng, shape, width, limit, cuts=(), kind=jnp.bfloat16):
    level = shard_levels(rng, shape, cuts, -0.22, 0.18) if cuts else 1.0
    result = jax.random.normal(rng, shape, jnp.float32) * width * level
    return jnp.minimum(jnp.maximum(result, -limit), limit).astype(kind)


def setup_inputs(seed: int = 0) -> dict:
    arg_keys = jax.random.split(jax.random.key(seed), 14)
    tokens = centred(arg_keys[0], (TOKENS, D), 1.0, 6.0, ((0, 32),))
    attn_gain = jnp.clip(1.0 + 0.1 * jax.random.normal(arg_keys[1], (D,), jnp.float32), 0.5, 1.5).astype(jnp.bfloat16)
    qkv_weight = centred(arg_keys[2], (D, 3 * D), D ** -0.5, 0.21875, ((0, 32),))
    out_weight = centred(arg_keys[3], (D, D), (D // 32) ** -0.5, 1.25, ((0, 32),))
    ffn_gain = jnp.clip(1.0 + 0.1 * jax.random.normal(arg_keys[4], (D,), jnp.float32), 0.5, 1.5).astype(jnp.bfloat16)
    router_weight = centred(arg_keys[5], (D, EXPERTS), (2 * D) ** -0.5, 0.15625, ((0, 32),))
    expert_in = centred(arg_keys[6], (EXPERTS, D, FF), D ** -0.5, 0.21875, ((0, 8), (1, 4)))
    expert_out = centred(arg_keys[7], (EXPERTS, FF, D), (FF // 2) ** -0.5, 0.15625, ((0, 8), (1, 4)))
    bias_table = centred(arg_keys[8], (HEADS, BUCKETS), 1.0, 4.0, (), jnp.float32)
    seq_lengths = jax.vmap(lambda own: uneven(own, SEQ_DEV, TOK_DEV, MAXLEN, 2))(jax.random.split(arg_keys[9], DEVICES)).reshape((DEVICES, SEQ_DEV)).astype(jnp.int32)
    bucket_map = with_ends(jax.random.randint(arg_keys[10], (MAXLEN,), 0, BUCKETS), jax.random.fold_in(arg_keys[10], 1), 0, BUCKETS - 1).astype(jnp.int32)
    expert_ids_keys = jax.random.split(jax.random.fold_in(arg_keys[11], 1), TOKENS // TOK_DEV)
    expert_ids_turns = jax.random.permutation(jax.random.fold_in(arg_keys[11], 3), TOKENS // TOK_DEV)
    expert_ids = jax.vmap(lambda own, number: assign_block(jax.random.fold_in(arg_keys[11], 2), own, number, TOK_DEV, EXPERTS, 2, CAP, 2))(expert_ids_keys, expert_ids_turns).reshape((TOKENS, 2))
    cotangent = centred(arg_keys[12], (TOKENS, D), 1.0, 6.0, ((0, 32),))
    return {"tokens": tokens, "attn_gain": attn_gain, "qkv_weight": qkv_weight, "out_weight": out_weight, "ffn_gain": ffn_gain, "router_weight": router_weight, "expert_in": expert_in, "expert_out": expert_out, "bias_table": bias_table, "seq_lengths": seq_lengths, "bucket_map": bucket_map, "expert_ids": expert_ids, "cotangent": cotangent}


EPSILON = 1e-06
MASKED = -1e+30
GELU_COEF = 0.7978845608028654

@jax.custom_vjp
def low(v):
    return lax.optimization_barrier(v.astype(jnp.bfloat16)).astype(jnp.float32)

@jax.custom_vjp
def low_back(v):
    return v

def low_keep(v):
    return (low(v), None)

def low_pass(kept, grad):
    return (grad,)

def back_keep(v):
    return (v, None)

def back_low(kept, grad):
    return (low(grad),)
low.defvjp(low_keep, low_pass)
low_back.defvjp(back_keep, back_low)

def rms_norm(values, gain_vector):
    return values * lax.rsqrt(lax.optimization_barrier(jnp.mean(values * values, axis=-1, keepdims=True)) + EPSILON) * gain_vector

def smooth_gelu(values):
    return 0.5 * values * (1.0 + jnp.tanh(GELU_COEF * (values + 0.044715 * values * values * values)))

def layout(lengths, bucket_map, row_count):
    seq_ends = jnp.cumsum(lengths, dtype=jnp.int32)
    places = jnp.arange(row_count, dtype=jnp.int32)
    segment = lax.optimization_barrier(jnp.sum((places[:, None] >= seq_ends[None, :]).astype(jnp.int32), axis=1, dtype=jnp.int32))
    offset = places[:, None] - places[None, :]
    allowed = (segment[:, None] == segment[None, :]) & (offset >= 0)
    clipped = jnp.clip(offset, 0, bucket_map.shape[0] - 1).astype(jnp.int32)
    return (allowed, jnp.take(bucket_map, clipped, axis=0))

def slot_position(device_ids, experts):
    flat_ids = device_ids.reshape(-1)
    chosen = (flat_ids[:, None] == jnp.arange(experts, dtype=jnp.int32)[None, :]).astype(jnp.int32)
    before = jnp.cumsum(chosen, axis=0, dtype=jnp.int32) - chosen
    position = lax.optimization_barrier(jnp.sum(before * chosen, axis=1, dtype=jnp.int32))
    return position.reshape(device_ids.shape)

def forward(tokens, attn_gain, qkv_weight, out_weight, ffn_gain, router_weight, expert_in, expert_out, bias_table, seq_lengths, bucket_map, expert_ids):
    highest = lax.Precision.HIGHEST
    devices = N_FSDP * N_REP
    score_scale = HEAD_DIM ** (-0.5)

    def attend(block_pair):
        row_block, lengths = block_pair
        allowed, bucket_index = layout(lengths, bucket_map, TOK_DEV)
        normed = low(rms_norm(row_block, attn_gain))
        packed = low(low_back(jnp.dot(normed, qkv_weight, precision=highest)))
        queries = packed[:, :D].reshape(TOK_DEV, HEADS, HEAD_DIM)
        keys_all = packed[:, D:2 * D].reshape(TOK_DEV, HEADS, HEAD_DIM)
        values_all = packed[:, 2 * D:].reshape(TOK_DEV, HEADS, HEAD_DIM)
        raw_score = jnp.einsum('ihd,jhd->hij', queries, keys_all, precision=highest)
        score = low_back(raw_score * score_scale + jnp.take(bias_table, bucket_index, axis=1))
        score = jnp.where(allowed[None], score, MASKED)
        row_peak = lax.optimization_barrier(jnp.max(score, axis=-1, keepdims=True))
        exponent = jnp.exp(score - row_peak)
        attn_probs = low(exponent / lax.optimization_barrier(jnp.sum(exponent, axis=-1, keepdims=True)))
        attended = jnp.einsum('hij,jhd->ihd', attn_probs, values_all, precision=highest).reshape(TOK_DEV, D)
        attended = low(low_back(attended))
        return row_block + low_back(jnp.dot(attended, out_weight, precision=highest))
    mixed_rows = lax.map(jax.checkpoint(attend), (tokens.reshape(devices, TOK_DEV, D), seq_lengths)).reshape(TOKENS, D)
    normed_two = low(rms_norm(mixed_rows, ffn_gain))
    logits = low_back(jnp.dot(normed_two, router_weight, precision=highest))
    choose = expert_ids[:, :, None] == jnp.arange(EXPERTS, dtype=jnp.int32)[None, None, :]
    picked = lax.optimization_barrier(jnp.sum(jnp.where(choose, logits[:, None, :], 0.0), axis=2))
    gate_exp = jnp.exp(picked - lax.optimization_barrier(jnp.max(picked, axis=1, keepdims=True)))
    gate_values = gate_exp / lax.optimization_barrier(jnp.sum(gate_exp, axis=1, keepdims=True))
    position = jax.vmap(lambda device_ids: slot_position(device_ids, EXPERTS))(expert_ids.reshape(devices, TOK_DEV, 2))
    column = (jnp.arange(devices, dtype=jnp.int32)[:, None, None] * CAP + position).reshape(TOKENS, 2).astype(jnp.int32)
    buffer = jnp.zeros((EXPERTS, devices * CAP, D), jnp.float32)
    buffer = buffer.at[expert_ids[:, 0], column[:, 0]].set(normed_two)
    buffer = low_back(buffer.at[expert_ids[:, 1], column[:, 1]].set(normed_two))

    def expert(expert_triple):
        expert_rows, first_weight, second_weight = expert_triple
        hidden = low_back(jnp.dot(expert_rows, first_weight, precision=highest))
        active = low(smooth_gelu(hidden))
        return low(low_back(jnp.dot(active, second_weight, precision=highest)))
    produced = lax.map(jax.checkpoint(expert), (buffer, expert_in, expert_out))
    first_out = produced[expert_ids[:, 0], column[:, 0]]
    second_out = produced[expert_ids[:, 1], column[:, 1]]
    return mixed_rows + gate_values[:, 0:1] * first_out + gate_values[:, 1:2] * second_out

def reference(tokens, attn_gain, qkv_weight, out_weight, ffn_gain, router_weight, expert_in, expert_out, bias_table, seq_lengths, bucket_map, expert_ids, cotangent):
    floats = (tokens.astype(jnp.float32), attn_gain.astype(jnp.float32), qkv_weight.astype(jnp.float32), out_weight.astype(jnp.float32), ffn_gain.astype(jnp.float32), router_weight.astype(jnp.float32), expert_in.astype(jnp.float32), expert_out.astype(jnp.float32), bias_table.astype(jnp.float32))

    def wrapped(*weights):
        return forward(*weights, seq_lengths, bucket_map, expert_ids)
    output, pull_back = jax.vjp(wrapped, *floats)
    gradients = pull_back(cotangent.astype(jnp.float32))
    return (output.astype(jnp.bfloat16), gradients[0], gradients[1], gradients[2], gradients[3], gradients[4], gradients[5], gradients[6], gradients[7], gradients[8])
```

```python
import functools

import jax
import jax.numpy as jnp
from jax import lax
from jax.experimental import pallas as pl
from jax.experimental.pallas import tpu as pltpu
from jax.sharding import PartitionSpec as P

EPSILON = 1e-06
MASKED = -1e30
GELU_COEF = 0.7978845608028654
TILE = 128
LANES = 128
VMEM_BYTES = 56 * 1024 * 1024


def rms_norm(values, gain_vector):
    return (
        values
        * lax.rsqrt(jnp.mean(values * values, axis=-1, keepdims=True) + EPSILON)
        * gain_vector
    )


def times(left_side, right_side):
    return lax.dot_general(
        left_side, right_side, (((1,), (0,)), ((), ())), preferred_element_type=jnp.float32
    )


def times_trans(left_side, right_side):
    return lax.dot_general(
        left_side, right_side, (((1,), (1,)), ((), ())), preferred_element_type=jnp.float32
    )


def trans_times(left_side, right_side):
    return lax.dot_general(
        left_side, right_side, (((0,), (0,)), ((), ())), preferred_element_type=jnp.float32
    )


def sequence_starts(lengths, row_count):
    seq_ends = jnp.cumsum(lengths, dtype=jnp.int32)
    places = jnp.arange(row_count, dtype=jnp.int32)
    passed = places[:, None] >= seq_ends[None, :]
    return jnp.max(jnp.where(passed, seq_ends[None, :], 0), axis=1, keepdims=True)


def distance_onehot(bucket_map, row_count, buckets):
    longest = bucket_map.shape[0]
    distance = row_count - TILE - jnp.arange(row_count, dtype=jnp.int32)
    place = jnp.arange(longest, dtype=jnp.int32)
    at_distance = jnp.sum(
        jnp.where(distance[:, None] == place[None, :], bucket_map[None, :] + 1, 0), axis=1
    )
    return (at_distance[:, None] == 1 + jnp.arange(buckets, dtype=jnp.int32)[None, :]).astype(
        jnp.float32
    )


def head_lanes(block, which, head_size):
    lane = lax.broadcasted_iota(jnp.int32, block.shape, 1)
    inside = (lane >= which * head_size) & (lane < (which + 1) * head_size)
    return jnp.where(inside, block, jnp.zeros_like(block))


def bias_strip(base_ref, head, row_count):
    row = base_ref[pl.ds(head, 1), :]
    spread = jnp.broadcast_to(row, (TILE, row_count))
    return pltpu.roll(spread, 0, 1, stride=1, stride_axis=0)


def tile_probs(query_tile, keys, strip, starts, tile, scale):
    row_count = strip.shape[1]
    width = TILE * (tile + 1)
    score = times_trans(query_tile, keys[:width]) * scale + strip[:, row_count - width :]
    place = lax.broadcasted_iota(jnp.int32, score.shape, 1)
    row = lax.broadcasted_iota(jnp.int32, score.shape, 0) + TILE * tile
    score = jnp.where((place <= row) & (place >= starts), score, MASKED)
    exponent = jnp.exp(score - jnp.max(score, axis=1, keepdims=True))
    return exponent * (1.0 / jnp.sum(exponent, axis=1, keepdims=True))


def lane_block(first):
    return pl.ds(pl.multiple_of(first, LANES), LANES)


def attention_kernel(head_size, base_ref, starts_ref, packed_ref, attended_ref):
    row_count, width = attended_ref.shape
    per_block = LANES // head_size
    scale = head_size ** (-0.5)

    @pl.loop(0, width // LANES)
    def _(block):
        queries = packed_ref[:, lane_block(block * LANES)]
        keys = packed_ref[:, lane_block(width + block * LANES)]
        values = packed_ref[:, lane_block(2 * width + block * LANES)]
        strips = [bias_strip(base_ref, block * per_block + own, row_count) for own in range(per_block)]
        for tile in range(row_count // TILE):
            rows = slice(tile * TILE, (tile + 1) * TILE)
            starts = starts_ref[rows, :]
            total = jnp.zeros((TILE, LANES), jnp.float32)
            for own in range(per_block):
                probs = tile_probs(
                    head_lanes(queries[rows], own, head_size), keys, strips[own], starts, tile, scale
                ).astype(jnp.bfloat16)
                total += times(probs, head_lanes(values[: probs.shape[1]], own, head_size))
            attended_ref[rows, lane_block(block * LANES)] = total.astype(jnp.bfloat16)


def attention(base, starts, packed, head_size):
    row_count = packed.shape[0]
    width = packed.shape[1] // 3
    return pl.pallas_call(
        functools.partial(attention_kernel, head_size),
        out_shape=jax.ShapeDtypeStruct((row_count, width), jnp.bfloat16),
        compiler_params=pltpu.CompilerParams(vmem_limit_bytes=VMEM_BYTES),
        cost_estimate=pl.CostEstimate(
            flops=8 * row_count * row_count * width,
            bytes_accessed=8 * row_count * width,
            transcendentals=row_count * row_count * width // head_size,
        ),
        name="attention",
    )(base, starts, packed)


def attention_pull_kernel(
    head_size,
    base_ref,
    starts_ref,
    packed_ref,
    grad_ref,
    d_packed_ref,
    d_base_ref,
    d_keys_ref,
    d_values_ref,
    d_strip_ref,
):
    row_count, width = grad_ref.shape
    per_block = LANES // head_size
    scale = head_size ** (-0.5)

    @pl.loop(0, width // LANES)
    def _(block):
        queries = packed_ref[:, lane_block(block * LANES)]
        keys = packed_ref[:, lane_block(width + block * LANES)]
        values = packed_ref[:, lane_block(2 * width + block * LANES)]
        grads = grad_ref[:, lane_block(block * LANES)]
        strips = [bias_strip(base_ref, block * per_block + own, row_count) for own in range(per_block)]
        d_keys_ref[...] = jnp.zeros_like(d_keys_ref)
        d_values_ref[...] = jnp.zeros_like(d_values_ref)
        d_strip_ref[...] = jnp.zeros_like(d_strip_ref)
        for tile in range(row_count // TILE):
            rows = slice(tile * TILE, (tile + 1) * TILE)
            reach = TILE * (tile + 1)
            starts = starts_ref[rows, :]
            d_queries = jnp.zeros((TILE, LANES), jnp.float32)
            for own in range(per_block):
                own_queries = head_lanes(queries[rows], own, head_size)
                own_grads = head_lanes(grads[rows], own, head_size)
                probs = tile_probs(own_queries, keys, strips[own], starts, tile, scale)
                d_probs = times_trans(own_grads, values[:reach])
                row_delta = jnp.sum(probs * d_probs, axis=1, keepdims=True)
                d_score = (probs * (d_probs - row_delta)).astype(jnp.bfloat16)
                d_strip_ref[own, :, row_count - reach :] += d_score.astype(jnp.float32)
                d_queries += times(d_score, head_lanes(keys[:reach], own, head_size))
                d_keys_ref[:reach, :] += trans_times(d_score, own_queries)
                d_values_ref[:reach, :] += trans_times(probs.astype(jnp.bfloat16), own_grads)
            d_packed_ref[rows, lane_block(block * LANES)] = (d_queries * scale).astype(jnp.bfloat16)
        d_packed_ref[:, lane_block(width + block * LANES)] = (d_keys_ref[...] * scale).astype(
            jnp.bfloat16
        )
        d_packed_ref[:, lane_block(2 * width + block * LANES)] = d_values_ref[...].astype(
            jnp.bfloat16
        )
        for own in range(per_block):
            folded = d_strip_ref[own]
            half = TILE // 2
            while half >= 8:
                folded = folded[:half] + pltpu.roll(folded[half:], row_count - half, 1)
                half //= 2
            row = lax.broadcasted_iota(jnp.int32, folded.shape, 0)
            for bit in (4, 2, 1):
                folded = jnp.where(
                    (row & bit) != 0, pltpu.roll(folded, row_count - bit, 1), folded
                )
            d_base_ref[pl.ds(block * per_block + own, 1), :] = jnp.sum(
                folded, axis=0, keepdims=True
            )


def attention_pull(base, starts, packed, grads, head_size):
    row_count, width = grads.shape
    return pl.pallas_call(
        functools.partial(attention_pull_kernel, head_size),
        out_shape=(
            jax.ShapeDtypeStruct(packed.shape, jnp.bfloat16),
            jax.ShapeDtypeStruct(base.shape, jnp.float32),
        ),
        scratch_shapes=[
            pltpu.VMEM((row_count, LANES), jnp.float32),
            pltpu.VMEM((row_count, LANES), jnp.float32),
            pltpu.VMEM((LANES // head_size, TILE, row_count), jnp.float32),
        ],
        compiler_params=pltpu.CompilerParams(vmem_limit_bytes=VMEM_BYTES),
        cost_estimate=pl.CostEstimate(
            flops=20 * row_count * row_count * width,
            bytes_accessed=14 * row_count * width,
            transcendentals=row_count * row_count * width // head_size,
        ),
        name="attention_pull",
    )(base, starts, packed, grads)


def gelu_parts(values):
    inner = GELU_COEF * (values + 0.044715 * values * values * values)
    bend = jnp.tanh(inner)
    slope = 0.5 * (1.0 + bend) + 0.5 * values * (1.0 - bend * bend) * (
        GELU_COEF * (1.0 + 3.0 * 0.044715 * values * values)
    )
    return 0.5 * values * (1.0 + bend), slope


def expert_rows_kernel(
    chunk,
    own_ref,
    rows_ref,
    grads_ref,
    other_ref,
    router_ref,
    in_ref,
    out_ref,
    produced_ref,
    active_ref,
    d_hidden_ref,
    slot_grad_ref,
    row_grad_ref,
    d_gate_ref,
    produced_sum,
    row_sum,
):
    hidden_width = in_ref.shape[1]
    rows = rows_ref[...]
    logits = times(rows, router_ref[...])
    column = lax.broadcasted_iota(jnp.int32, logits.shape, 1)
    own_logit = jnp.sum(jnp.where(column == own_ref[0], logits, 0.0), axis=1, keepdims=True)
    other_logit = jnp.sum(jnp.where(column == other_ref[...], logits, 0.0), axis=1, keepdims=True)
    peak = jnp.maximum(own_logit, other_logit)
    own_part = jnp.exp(own_logit - peak)
    gate = own_part / (own_part + jnp.exp(other_logit - peak))
    grads = grads_ref[...].astype(jnp.float32)
    slot_grad_ref[...] = (gate * grads).astype(jnp.bfloat16)
    for step in range(hidden_width // chunk):
        columns = slice(step * chunk, (step + 1) * chunk)
        hidden = times(rows_ref[...], in_ref[:, columns])
        active, slope = gelu_parts(hidden)
        active = active.astype(jnp.bfloat16)
        active_ref[:, columns] = active
        d_active = times_trans(slot_grad_ref[...], out_ref[columns, :])
        d_hidden = (slope * d_active).astype(jnp.bfloat16)
        d_hidden_ref[:, columns] = d_hidden
        produced = times(active, out_ref[columns, :])
        back = times_trans(d_hidden, in_ref[:, columns])
        if step == 0:
            produced_sum[...] = produced
            row_sum[...] = back
        else:
            produced_sum[...] += produced
            row_sum[...] += back
    result = produced_sum[...].astype(jnp.bfloat16)
    produced_ref[...] = result
    row_grad_ref[...] = row_sum[...].astype(jnp.bfloat16)
    d_gate_ref[...] = jnp.sum(result.astype(jnp.float32) * grads, axis=1, keepdims=True)


def expert_rows(own, rows, grads, other, router, weight_in, weight_out):
    row_count, width = rows.shape
    hidden_width = weight_in.shape[1]
    block = min(512, row_count)
    chunk = min(768, hidden_width)

    def by_rows(columns):
        return pl.BlockSpec((block, columns), lambda i: (i, 0))

    def whole(shape):
        return pl.BlockSpec(shape, lambda i: (0, 0), pipeline_mode=pl.Buffered(1))

    def like(columns, dtype=jnp.bfloat16):
        return jax.ShapeDtypeStruct((row_count, columns), dtype)

    return pl.pallas_call(
        functools.partial(expert_rows_kernel, chunk),
        grid=(row_count // block,),
        in_specs=[
            pl.BlockSpec(memory_space=pltpu.SMEM),
            by_rows(width),
            by_rows(width),
            by_rows(1),
            whole(router.shape),
            whole(weight_in.shape),
            whole(weight_out.shape),
        ],
        out_specs=(
            by_rows(width),
            by_rows(hidden_width),
            by_rows(hidden_width),
            by_rows(width),
            by_rows(width),
            by_rows(1),
        ),
        out_shape=(
            like(width),
            like(hidden_width),
            like(hidden_width),
            like(width),
            like(width),
            like(1, jnp.float32),
        ),
        scratch_shapes=[
            pltpu.VMEM((block, width), jnp.float32),
            pltpu.VMEM((block, width), jnp.float32),
        ],
        compiler_params=pltpu.CompilerParams(vmem_limit_bytes=VMEM_BYTES),
        cost_estimate=pl.CostEstimate(
            flops=8 * row_count * width * hidden_width,
            bytes_accessed=4 * row_count * (hidden_width + 3 * width) + 4 * width * hidden_width,
            transcendentals=row_count * hidden_width,
        ),
        name="expert_rows",
    )(own, rows, grads, other, router, weight_in, weight_out)


def slot_position(device_ids, experts):
    flat_ids = device_ids.reshape(-1)
    chosen = (flat_ids[:, None] == jnp.arange(experts, dtype=jnp.int32)[None, :]).astype(jnp.int32)
    before = jnp.cumsum(chosen, axis=0, dtype=jnp.int32) - chosen
    position = jnp.sum(before * chosen, axis=1, dtype=jnp.int32)
    return position.reshape(device_ids.shape)


def partner(size, step):
    return [(index, index ^ step) for index in range(size)]


def swap_blocks(blocks, axis, size):
    if size > 8:
        order = lax.axis_index(axis) ^ jnp.arange(size, dtype=jnp.int32)
        placed = jnp.take(jnp.stack(blocks), order, axis=0)
        landed = lax.all_to_all(placed, axis, split_axis=0, concat_axis=0, tiled=True)
        landed = jnp.take(landed, order, axis=0)
        return [landed[step] for step in range(size)]
    return [blocks[0]] + [
        lax.ppermute(blocks[step], axis, partner(size, step)) for step in range(1, size)
    ]


def gather_rep(shard, size):
    near = lax.ppermute(shard, "rep", partner(size, 1))
    far = lax.ppermute(shard, "rep", partner(size, 2))
    far_near = lax.ppermute(far, "rep", partner(size, 1))
    return place_rep([shard, near, far, far_near], lax.axis_index("rep"))


def place_rep(pieces, me):
    height, width = pieces[0].shape
    whole = jnp.zeros((len(pieces) * height, width), pieces[0].dtype)
    for step, piece in enumerate(pieces):
        whole = lax.dynamic_update_slice(whole, piece, ((me ^ step) * height, 0))
    return whole


def scatter_rep(piece_of, size):
    me = lax.axis_index("rep")
    near = lax.ppermute(piece_of(me ^ 1).astype(jnp.bfloat16), "rep", partner(size, 1))
    far_near = lax.ppermute(piece_of(me ^ 3).astype(jnp.bfloat16), "rep", partner(size, 1))
    far = (piece_of(me ^ 2) + far_near.astype(jnp.float32)).astype(jnp.bfloat16)
    far = lax.ppermute(far, "rep", partner(size, 2))
    return piece_of(me) + near.astype(jnp.float32) + far.astype(jnp.float32)


def shards(
    fsdp,
    rep,
    tokens,
    attn_gain,
    qkv_weight,
    out_weight,
    ffn_gain,
    router_weight,
    expert_in,
    expert_out,
    bias_table,
    seq_lengths,
    bucket_map,
    expert_ids,
    cotangent,
):
    both = ("fsdp", "rep")
    row_count, model_width = tokens.shape
    head_count, buckets = bias_table.shape
    head_size = model_width // head_count
    experts = router_weight.shape[1]
    capacity = 4 * row_count // experts
    highest = lax.Precision.HIGHEST
    own_rows = qkv_weight.shape[0]
    extra = -(-(experts + 2) // LANES) * LANES
    me = lax.axis_index("fsdp")

    small = jnp.concatenate(
        [
            router_weight,
            attn_gain[:, None],
            ffn_gain[:, None],
            jnp.zeros((own_rows, extra - experts - 2), jnp.bfloat16),
        ],
        axis=1,
    )
    first_part = lax.all_gather(
        jnp.concatenate([qkv_weight, small], axis=1), both, axis=0, tiled=True
    )
    weight_out = lax.all_gather(out_weight, both, axis=0, tiled=True)
    weight_in = gather_rep(expert_in[0], rep)
    weight_back = gather_rep(expert_out[0], rep)

    position = slot_position(expert_ids, experts)
    slot_ids = (expert_ids ^ me) * capacity + position
    slot_rows = jnp.arange(experts * capacity, dtype=jnp.int32)
    in_first = slot_rows[:, None] == slot_ids[None, :, 0]
    in_second = slot_rows[:, None] == slot_ids[None, :, 1]
    first_map = in_first.astype(jnp.bfloat16)
    second_map = in_second.astype(jnp.bfloat16)
    dispatch = first_map + second_map
    others = jnp.sum(
        jnp.where(in_first, expert_ids[None, :, 1], 0)
        + jnp.where(in_second, expert_ids[None, :, 0], 0),
        axis=1,
    )

    def to_blocks(rows):
        return [rows[step * capacity : (step + 1) * capacity] for step in range(experts)]

    slot_others = jnp.concatenate(swap_blocks(to_blocks(others), "fsdp", fsdp))[:, None]
    sent_grads = times(dispatch, cotangent).astype(jnp.bfloat16)
    slot_dy = jnp.concatenate(swap_blocks(to_blocks(sent_grads), "fsdp", fsdp))

    weight_qkv = first_part[:, : qkv_weight.shape[1]]
    small = first_part[:, qkv_weight.shape[1] :]
    weight_router = small[:, :experts]
    gain_one = small[:, experts].astype(jnp.float32)
    gain_two = small[:, experts + 1].astype(jnp.float32)

    onehot = distance_onehot(bucket_map, row_count, buckets)
    base = lax.dot_general(bias_table, onehot, (((1,), (1,)), ((), ())), precision=highest)
    starts = sequence_starts(seq_lengths[0], row_count)
    inputs = tokens.astype(jnp.float32)
    normed_one = rms_norm(inputs, gain_one).astype(jnp.bfloat16)
    packed = times(normed_one, weight_qkv).astype(jnp.bfloat16)
    attended = attention(base, starts, packed, head_size)
    mixed_rows = inputs + times(attended, weight_out)
    normed_two = rms_norm(mixed_rows, gain_two).astype(jnp.bfloat16)

    sending = times(dispatch, normed_two).astype(jnp.bfloat16)
    arrived = jnp.concatenate(swap_blocks(to_blocks(sending), "fsdp", fsdp))
    produced, active, d_hidden, slot_grad, row_grads, slot_d_gates = expert_rows(
        me[None].astype(jnp.int32), arrived, slot_dy, slot_others, small, weight_in, weight_back
    )
    back_rows = jnp.concatenate(swap_blocks(to_blocks(row_grads), "fsdp", fsdp))
    back_gates = jnp.concatenate(swap_blocks(to_blocks(slot_d_gates[:, 0]), "fsdp", fsdp))
    returned = jnp.concatenate(swap_blocks(to_blocks(produced), "fsdp", fsdp))

    in_rows = expert_in.shape[1]
    out_rows = expert_out.shape[1]
    owned_in = scatter_rep(
        lambda who: trans_times(
            lax.dynamic_slice_in_dim(arrived, who * in_rows, in_rows, 1), d_hidden
        ),
        rep,
    )
    owned_out = scatter_rep(
        lambda who: trans_times(
            lax.dynamic_slice_in_dim(active, who * out_rows, out_rows, 1), slot_grad
        ),
        rep,
    )

    logits = times(normed_two, weight_router)
    choose = expert_ids[:, :, None] == jnp.arange(experts, dtype=jnp.int32)[None, None, :]
    picked = jnp.sum(jnp.where(choose, logits[:, None, :], 0.0), axis=2)
    gate_exp = jnp.exp(picked - jnp.max(picked, axis=1, keepdims=True))
    gate_values = gate_exp / jnp.sum(gate_exp, axis=1, keepdims=True)
    d_gates = jnp.stack(
        [
            jnp.sum(jnp.where(in_first, back_gates[:, None], 0.0), axis=0),
            jnp.sum(jnp.where(in_second, back_gates[:, None], 0.0), axis=0),
        ],
        axis=1,
    )
    gate_mean = jnp.sum(gate_values * d_gates, axis=1, keepdims=True)
    d_picked = gate_values * (d_gates - gate_mean)
    d_logits = jnp.sum(jnp.where(choose, d_picked[:, :, None], 0.0), axis=1).astype(jnp.bfloat16)
    d_normed_two = trans_times(dispatch, back_rows) + times_trans(d_logits, weight_router)
    grad_router = trans_times(normed_two, d_logits)
    unused_two, norm_pull_two = jax.vjp(rms_norm, mixed_rows, gain_two)
    d_mixed_norm, grad_gain_two = norm_pull_two(d_normed_two)
    d_mixed = cotangent.astype(jnp.float32) + d_mixed_norm
    d_branch = d_mixed.astype(jnp.bfloat16)
    grad_out_weight = trans_times(attended, d_branch)
    owned_early = lax.psum_scatter(
        jnp.concatenate(
            [
                grad_out_weight,
                grad_router,
                grad_gain_two[:, None],
                jnp.zeros((model_width, extra - experts - 1), jnp.float32),
            ],
            axis=1,
        ),
        both,
        scatter_dimension=0,
        tiled=True,
    )
    d_attended = times_trans(d_branch, weight_out).astype(jnp.bfloat16)
    d_packed, d_base = attention_pull(base, starts, packed, d_attended, head_size)
    bias_grad = lax.psum(jnp.dot(d_base, onehot, precision=highest), both)
    grad_qkv = trans_times(normed_one, d_packed)
    d_normed_one = times_trans(d_packed, weight_qkv)
    unused_one, norm_pull_one = jax.vjp(rms_norm, inputs, gain_one)
    d_inputs_norm, grad_gain_one = norm_pull_one(d_normed_one)
    token_grad = d_mixed + d_inputs_norm
    owned_late = lax.psum_scatter(
        jnp.concatenate(
            [
                grad_qkv,
                grad_gain_one[:, None],
                jnp.zeros((model_width, LANES - 1), jnp.float32),
            ],
            axis=1,
        ),
        both,
        scatter_dimension=0,
        tiled=True,
    )
    first_out = trans_times(first_map, returned)
    second_out = trans_times(second_map, returned)
    output = mixed_rows + gate_values[:, 0:1] * first_out + gate_values[:, 1:2] * second_out
    qkv_width = qkv_weight.shape[1]
    return (
        output.astype(jnp.bfloat16),
        token_grad,
        owned_late[:, qkv_width],
        owned_late[:, :qkv_width],
        owned_early[:, :model_width],
        owned_early[:, model_width + experts],
        owned_early[:, model_width : model_width + experts],
        owned_in[None],
        owned_out[None],
        bias_grad,
    )


def solution(mesh):
    return jax.shard_map(
        functools.partial(shards, mesh.shape["fsdp"], mesh.shape["rep"]),
        mesh=mesh,
        in_specs=(
            P(("fsdp", "rep"), None),
            P(("fsdp", "rep")),
            P(("fsdp", "rep"), None),
            P(("fsdp", "rep"), None),
            P(("fsdp", "rep")),
            P(("fsdp", "rep"), None),
            P("fsdp", "rep", None),
            P("fsdp", "rep", None),
            P(),
            P(("fsdp", "rep"), None),
            P(),
            P(("fsdp", "rep"), None),
            P(("fsdp", "rep"), None),
        ),
        out_specs=(
            P(("fsdp", "rep"), None),
            P(("fsdp", "rep"), None),
            P(("fsdp", "rep")),
            P(("fsdp", "rep"), None),
            P(("fsdp", "rep"), None),
            P(("fsdp", "rep")),
            P(("fsdp", "rep"), None),
            P("fsdp", "rep", None),
            P("fsdp", "rep", None),
            P(),
        ),
        check_vma=False,
    )
```

```python
import functools

import jax
import jax.numpy as jnp
from jax import lax
from jax.experimental import pallas as pl
from jax.experimental.pallas import tpu as pltpu
from jax.sharding import PartitionSpec as P

EPSILON = 1e-06
MASKED = -1e30
GELU_COEF = 0.7978845608028654
TILE = 128
LANES = 128
PARTS = 2
TAIL = 16
VMEM_BYTES = 56 * 1024 * 1024


def rms_norm(values, gain_vector):
    return (
        values
        * lax.rsqrt(jnp.mean(values * values, axis=-1, keepdims=True) + EPSILON)
        * gain_vector
    )


def times(left_side, right_side):
    return lax.dot_general(
        left_side, right_side, (((1,), (0,)), ((), ())), preferred_element_type=jnp.float32
    )


def times_trans(left_side, right_side):
    return lax.dot_general(
        left_side, right_side, (((1,), (1,)), ((), ())), preferred_element_type=jnp.float32
    )


def trans_times(left_side, right_side):
    return lax.dot_general(
        left_side, right_side, (((0,), (0,)), ((), ())), preferred_element_type=jnp.float32
    )


def sequence_starts(lengths, row_count):
    seq_ends = jnp.cumsum(lengths, dtype=jnp.int32)
    places = jnp.arange(row_count, dtype=jnp.int32)
    passed = places[:, None] >= seq_ends[None, :]
    return jnp.max(jnp.where(passed, seq_ends[None, :], 0), axis=1, keepdims=True)


def distance_onehot(bucket_map, row_count, buckets):
    longest = bucket_map.shape[0]
    distance = row_count - TILE - jnp.arange(row_count, dtype=jnp.int32)
    place = jnp.arange(longest, dtype=jnp.int32)
    at_distance = jnp.sum(
        jnp.where(distance[:, None] == place[None, :], bucket_map[None, :] + 1, 0), axis=1
    )
    return (at_distance[:, None] == 1 + jnp.arange(buckets, dtype=jnp.int32)[None, :]).astype(
        jnp.float32
    )


def head_lanes(block, which, head_size):
    lane = lax.broadcasted_iota(jnp.int32, block.shape, 1)
    inside = (lane >= which * head_size) & (lane < (which + 1) * head_size)
    return jnp.where(inside, block, jnp.zeros_like(block))


def bias_strip(base_ref, head, row_count):
    row = base_ref[pl.ds(head, 1), :]
    spread = jnp.broadcast_to(row, (TILE, row_count))
    return pltpu.roll(spread, 0, 1, stride=1, stride_axis=0)


def tile_probs(query_tile, keys, strip, starts, tile, scale):
    row_count = strip.shape[1]
    width = TILE * (tile + 1)
    score = times_trans(query_tile, keys[:width]) * scale + strip[:, row_count - width :]
    place = lax.broadcasted_iota(jnp.int32, score.shape, 1)
    row = lax.broadcasted_iota(jnp.int32, score.shape, 0) + TILE * tile
    score = jnp.where((place <= row) & (place >= starts), score, MASKED)
    exponent = jnp.exp(score - jnp.max(score, axis=1, keepdims=True))
    return exponent * (1.0 / jnp.sum(exponent, axis=1, keepdims=True))


def lane_block(first):
    return pl.ds(pl.multiple_of(first, LANES), LANES)


def attention_kernel(head_size, base_ref, starts_ref, packed_ref, attended_ref):
    row_count, width = attended_ref.shape
    per_block = LANES // head_size
    scale = head_size ** (-0.5)

    @pl.loop(0, width // LANES)
    def _(block):
        queries = packed_ref[:, lane_block(block * LANES)]
        keys = packed_ref[:, lane_block(width + block * LANES)]
        values = packed_ref[:, lane_block(2 * width + block * LANES)]
        strips = [bias_strip(base_ref, block * per_block + own, row_count) for own in range(per_block)]
        for tile in range(row_count // TILE):
            rows = slice(tile * TILE, (tile + 1) * TILE)
            starts = starts_ref[rows, :]
            total = jnp.zeros((TILE, LANES), jnp.float32)
            for own in range(per_block):
                probs = tile_probs(
                    head_lanes(queries[rows], own, head_size), keys, strips[own], starts, tile, scale
                ).astype(jnp.bfloat16)
                total += times(probs, head_lanes(values[: probs.shape[1]], own, head_size))
            attended_ref[rows, lane_block(block * LANES)] = total.astype(jnp.bfloat16)


def attention(base, starts, packed, head_size):
    row_count = packed.shape[0]
    width = packed.shape[1] // 3
    return pl.pallas_call(
        functools.partial(attention_kernel, head_size),
        out_shape=jax.ShapeDtypeStruct((row_count, width), jnp.bfloat16),
        compiler_params=pltpu.CompilerParams(vmem_limit_bytes=VMEM_BYTES),
        cost_estimate=pl.CostEstimate(flops=1000, bytes_accessed=1000, transcendentals=0),
        name="attention",
    )(base, starts, packed)


def attention_pull_kernel(
    head_size,
    base_ref,
    starts_ref,
    packed_ref,
    grad_ref,
    kept_rows_ref,
    sent_rows_ref,
    d_packed_ref,
    d_base_ref,
    keep_ref,
    send_ref,
    d_keys_ref,
    d_values_ref,
    d_strip_ref,
):
    row_count, width = grad_ref.shape
    per_block = LANES // head_size
    scale = head_size ** (-0.5)

    @pl.loop(0, width // LANES)
    def _(block):
        queries = packed_ref[:, lane_block(block * LANES)]
        keys = packed_ref[:, lane_block(width + block * LANES)]
        values = packed_ref[:, lane_block(2 * width + block * LANES)]
        grads = grad_ref[:, lane_block(block * LANES)]
        strips = [bias_strip(base_ref, block * per_block + own, row_count) for own in range(per_block)]
        d_keys_ref[...] = jnp.zeros_like(d_keys_ref)
        d_values_ref[...] = jnp.zeros_like(d_values_ref)
        d_strip_ref[...] = jnp.zeros_like(d_strip_ref)
        for tile in range(row_count // TILE):
            rows = slice(tile * TILE, (tile + 1) * TILE)
            reach = TILE * (tile + 1)
            starts = starts_ref[rows, :]
            d_queries = jnp.zeros((TILE, LANES), jnp.float32)
            for own in range(per_block):
                own_queries = head_lanes(queries[rows], own, head_size)
                own_grads = head_lanes(grads[rows], own, head_size)
                probs = tile_probs(own_queries, keys, strips[own], starts, tile, scale)
                d_probs = times_trans(own_grads, values[:reach])
                row_delta = jnp.sum(probs * d_probs, axis=1, keepdims=True)
                d_score = (probs * (d_probs - row_delta)).astype(jnp.bfloat16)
                d_strip_ref[own, :, row_count - reach :] += d_score.astype(jnp.float32)
                d_queries += times(d_score, head_lanes(keys[:reach], own, head_size))
                d_keys_ref[:reach, :] += trans_times(d_score, own_queries)
                d_values_ref[:reach, :] += trans_times(probs.astype(jnp.bfloat16), own_grads)
            d_packed_ref[rows, lane_block(block * LANES)] = (d_queries * scale).astype(jnp.bfloat16)
        d_packed_ref[:, lane_block(width + block * LANES)] = (d_keys_ref[...] * scale).astype(
            jnp.bfloat16
        )
        d_packed_ref[:, lane_block(2 * width + block * LANES)] = d_values_ref[...].astype(
            jnp.bfloat16
        )
        for own in range(per_block):
            folded = d_strip_ref[own]
            half = TILE // 2
            while half >= 8:
                folded = folded[:half] + pltpu.roll(folded[half:], row_count - half, 1)
                half //= 2
            row = lax.broadcasted_iota(jnp.int32, folded.shape, 0)
            for bit in (4, 2, 1):
                folded = jnp.where(
                    (row & bit) != 0, pltpu.roll(folded, row_count - bit, 1), folded
                )
            d_base_ref[pl.ds(block * per_block + own, 1), :] = jnp.sum(
                folded, axis=0, keepdims=True
            )

    for start in range(0, 3 * width, width):
        columns = slice(start, start + width)
        send_ref[:, columns] = trans_times(sent_rows_ref[...], d_packed_ref[:, columns]).astype(
            jnp.bfloat16
        )
        keep_ref[:, columns] = trans_times(kept_rows_ref[...], d_packed_ref[:, columns])


def attention_pull(base, starts, packed, grads, rows, head_size):
    row_count, width = grads.shape
    half = rows[0].shape[1]
    return pl.pallas_call(
        functools.partial(attention_pull_kernel, head_size),
        out_shape=(
            jax.ShapeDtypeStruct(packed.shape, jnp.bfloat16),
            jax.ShapeDtypeStruct(base.shape, jnp.float32),
            jax.ShapeDtypeStruct((half, packed.shape[1]), jnp.float32),
            jax.ShapeDtypeStruct((half, packed.shape[1]), jnp.bfloat16),
        ),
        scratch_shapes=[
            pltpu.VMEM((row_count, LANES), jnp.float32),
            pltpu.VMEM((row_count, LANES), jnp.float32),
            pltpu.VMEM((LANES // head_size, TILE, row_count), jnp.float32),
        ],
        compiler_params=pltpu.CompilerParams(vmem_limit_bytes=VMEM_BYTES),
        cost_estimate=pl.CostEstimate(flops=1000, bytes_accessed=1000, transcendentals=0),
        name="attention_pull",
    )(base, starts, packed, grads, *rows)


def gelu_parts(values):
    inner = GELU_COEF * (values + 0.044715 * values * values * values)
    bend = jnp.tanh(inner)
    slope = 0.5 * (1.0 + bend) + 0.5 * values * (1.0 - bend * bend) * (
        GELU_COEF * (1.0 + 3.0 * 0.044715 * values * values)
    )
    return 0.5 * values * (1.0 + bend), slope


def vmem():
    return pl.BlockSpec(memory_space=pltpu.VMEM)


def two_gates(logits, first_ids, second_ids):
    column = lax.broadcasted_iota(jnp.int32, logits.shape, 1)
    first = jnp.sum(jnp.where(column == first_ids, logits, 0.0), axis=1, keepdims=True)
    second = jnp.sum(jnp.where(column == second_ids, logits, 0.0), axis=1, keepdims=True)
    peak = jnp.maximum(first, second)
    first, second = jnp.exp(first - peak), jnp.exp(second - peak)
    return first / (first + second), second / (first + second)


def project_kernel(column, tokens_ref, *refs):
    first_refs, second_refs = refs[0:2], refs[2:4]
    packed_ref, normed_refs = refs[4], refs[5:7]
    row_count, half = normed_refs[0].shape
    cut = first_refs[0].shape[1]
    rest = packed_ref.shape[1] - cut
    inputs = tokens_ref[...].astype(jnp.float32)
    inverse = lax.rsqrt(jnp.mean(inputs * inputs, axis=1, keepdims=True) + EPSILON)
    for which in range(2):
        small = second_refs[which][:, rest:].astype(jnp.float32)
        gain = jnp.transpose(small)[column : column + 1, :]
        normed = (inputs[:, which * half : (which + 1) * half] * inverse * gain).astype(
            jnp.bfloat16
        )
        normed_refs[which][...] = normed
    both = jnp.concatenate([normed_refs[0][...], normed_refs[1][...]], axis=1)
    for refs_of, start, width in ((first_refs, 0, cut), (second_refs, cut, rest)):
        weights = jnp.concatenate([refs_of[0][:, :width], refs_of[1][:, :width]], axis=0)
        packed_ref[:, start : start + width] = times(both, weights).astype(jnp.bfloat16)


def project(tokens_rel, first, second, column, qkv_width):
    row_count, width = tokens_rel.shape
    half = jax.ShapeDtypeStruct((row_count, width // 2), jnp.bfloat16)
    return pl.pallas_call(
        functools.partial(project_kernel, column),
        out_shape=(jax.ShapeDtypeStruct((row_count, qkv_width), jnp.bfloat16), half, half),
        compiler_params=pltpu.CompilerParams(vmem_limit_bytes=VMEM_BYTES),
        cost_estimate=pl.CostEstimate(flops=1000, bytes_accessed=1000, transcendentals=0),
        name="project",
    )(tokens_rel, *first, *second)


def slot_rows_of(ids_ref, rows, first_place, count):
    place = first_place + lax.broadcasted_iota(jnp.int32, (count, rows.shape[0]), 0)
    inside = (place == ids_ref[0:1, :]) | (place == ids_ref[1:2, :])
    return times(jnp.where(inside, 1.0, 0.0).astype(jnp.bfloat16), rows).astype(jnp.bfloat16)


def fill_blocks(ids_ref, rows, block_refs):
    experts, count, _ = block_refs[0].shape
    for part, block_ref in enumerate(block_refs):
        for expert in range(experts):
            place = (expert * len(block_refs) + part) * count
            block_ref[expert] = slot_rows_of(ids_ref, rows, place, count)


def spread_kernel(ids_ref, rows_ref, block_ref):
    fill_blocks(ids_ref, rows_ref[...], [block_ref])


def spread(slot_ids, rows, experts, capacity):
    row_count, width = rows.shape
    return pl.pallas_call(
        spread_kernel,
        out_shape=jax.ShapeDtypeStruct((experts, capacity, width), jnp.bfloat16),
        compiler_params=pltpu.CompilerParams(vmem_limit_bytes=VMEM_BYTES),
        cost_estimate=pl.CostEstimate(flops=1000, bytes_accessed=1000, transcendentals=0),
        name="spread",
    )(slot_ids, rows)


def mix_kernel(
    ids_ref, tokens_ref, attended_ref, out_ref, gain_ref, mixed_ref, normed_ref, *block_refs
):
    mixed = tokens_ref[...].astype(jnp.float32) + times(attended_ref[...], out_ref[...])
    mixed_ref[...] = mixed
    inverse = lax.rsqrt(jnp.mean(mixed * mixed, axis=1, keepdims=True) + EPSILON)
    normed_ref[...] = (mixed * inverse * gain_ref[...]).astype(jnp.bfloat16)
    fill_blocks(ids_ref, normed_ref[...], block_refs)


def mix(slot_ids, tokens, attended, weight_out, gain, experts, capacity):
    row_count, width = tokens.shape
    block = jax.ShapeDtypeStruct((experts, capacity // PARTS, width), jnp.bfloat16)
    return pl.pallas_call(
        mix_kernel,
        out_shape=(
            jax.ShapeDtypeStruct((row_count, width), jnp.float32),
            jax.ShapeDtypeStruct((row_count, width), jnp.bfloat16),
        )
        + (block,) * PARTS,
        compiler_params=pltpu.CompilerParams(vmem_limit_bytes=VMEM_BYTES),
        cost_estimate=pl.CostEstimate(flops=1000, bytes_accessed=1000, transcendentals=0),
        name="mix",
    )(slot_ids, tokens, attended, weight_out, gain)


def expert_kernel(
    place_ref,
    rows_ref,
    grads_ref,
    other_ref,
    router_ref,
    in_ref,
    out_ref,
    *refs,
):
    payload_ref, produced_ref, rows_all, slot_grad_all, active_ref, d_hidden_ref = refs[-10:-4]
    rows, slot_grad, produced_sum, row_sum = refs[-4:]
    sources, capacity, width = rows_ref.shape
    count = sources * capacity
    step = pl.program_id(0)

    @pl.when(step == 0)
    def _():
        rows[...] = rows_ref[...].reshape(count, width)
        logits = times(rows[...], router_ref[...])
        own_ids = jnp.full((count, 1), place_ref[0], jnp.int32)
        gate, unused_gate = two_gates(logits, own_ids, other_ref[...])
        grads = grads_ref[...].reshape(count, width).astype(jnp.float32)
        slot_grad[...] = (gate * grads).astype(jnp.bfloat16)
        rows_all[...] = rows[...]
        slot_grad_all[...] = slot_grad[...]
        produced_sum[...] = jnp.zeros_like(produced_sum)
        row_sum[...] = jnp.zeros_like(row_sum)

    hidden = times(rows[...], in_ref[...])
    active, slope = gelu_parts(hidden)
    active = active.astype(jnp.bfloat16)
    active_ref[...] = active
    d_active = times_trans(slot_grad[...], out_ref[...])
    d_hidden = (slope * d_active).astype(jnp.bfloat16)
    d_hidden_ref[...] = d_hidden
    produced_sum[...] += times(active, out_ref[...])
    row_sum[...] += times_trans(d_hidden, in_ref[...])

    @pl.when(step == pl.num_programs(0) - 1)
    def _():
        for source in range(sources):
            own = slice(source * capacity, (source + 1) * capacity)
            result = produced_sum[own, :].astype(jnp.bfloat16)
            produced_ref[source] = result
            payload_ref[source, :capacity, :] = row_sum[own, :].astype(jnp.bfloat16)
            d_gate = jnp.sum(
                result.astype(jnp.float32) * grads_ref[source].astype(jnp.float32),
                axis=1,
                keepdims=True,
            )
            across = jnp.transpose(jnp.broadcast_to(d_gate, (capacity, LANES)))[:TAIL, :]
            high = across.astype(jnp.bfloat16).astype(jnp.float32)
            row = lax.broadcasted_iota(jnp.int32, across.shape, 0)
            tail = jnp.where(row == 0, high, jnp.where(row == 1, across - high, 0.0))
            payload_ref[source, capacity:, :] = jnp.zeros((TAIL, width), jnp.bfloat16)
            payload_ref[source, capacity:, :capacity] = tail.astype(jnp.bfloat16)


def expert_rows(place, part, rows, grads, other, router, weight_in, weight_out, earlier):
    sources, capacity, width = rows.shape
    hidden_width = weight_in.shape[1]
    chunk = hidden_width // 4
    count = sources * capacity

    def whole(shape):
        return pl.BlockSpec(shape, lambda i, place: (0,) * len(shape))

    def part_of(*shape):
        return pl.BlockSpec(shape, lambda i, place: (0, part, 0))

    def part_block(columns):
        return pl.BlockSpec((count, columns), lambda i, place: (part, 0))

    def part_chunk():
        return pl.BlockSpec((count, chunk), lambda i, place: (part, i))

    def full(*shape):
        return jax.ShapeDtypeStruct(shape, jnp.bfloat16)

    total = PARTS * count
    operands = (rows, grads, other, router, weight_in, weight_out)
    in_specs = [
        whole(rows.shape),
        part_of(sources, capacity, width),
        whole(other.shape),
        whole(router.shape),
        pl.BlockSpec((width, chunk), lambda i, place: (0, i)),
        pl.BlockSpec((chunk, width), lambda i, place: (i, 0)),
    ]
    aliases = {}
    if earlier is not None:
        aliases = {1 + len(operands) + which: 1 + which for which in range(5)}
        operands = operands + tuple(earlier)
        in_specs = in_specs + [pl.BlockSpec(memory_space=pl.ANY)] * 5
    results = pl.pallas_call(
        expert_kernel,
        grid_spec=pltpu.PrefetchScalarGridSpec(
            num_scalar_prefetch=1,
            grid=(4,),
            in_specs=in_specs,
            out_specs=[
                whole((sources, capacity + TAIL, width)),
                part_of(sources, capacity, width),
                part_block(width),
                part_block(width),
                part_chunk(),
                part_chunk(),
            ],
            scratch_shapes=[
                pltpu.VMEM((count, width), jnp.bfloat16),
                pltpu.VMEM((count, width), jnp.bfloat16),
                pltpu.VMEM((count, width), jnp.float32),
                pltpu.VMEM((count, width), jnp.float32),
            ],
        ),
        out_shape=[
            full(sources, capacity + TAIL, width),
            full(sources, PARTS * capacity, width),
            full(total, width),
            full(total, width),
            full(total, hidden_width),
            full(total, hidden_width),
        ],
        input_output_aliases=aliases,
        compiler_params=pltpu.CompilerParams(vmem_limit_bytes=VMEM_BYTES),
        cost_estimate=pl.CostEstimate(
            flops=8 * count * width * hidden_width,
            bytes_accessed=4 * count * (hidden_width + 4 * width) + 4 * width * hidden_width,
            transcendentals=count * hidden_width,
        ),
        name="expert_rows",
    )(place, *operands)
    return results[0], results[1:]


def collect_kernel(
    slots_ref,
    experts_ref,
    places_ref,
    normed_ref,
    mixed_ref,
    cotangent_ref,
    router_ref,
    gain_ref,
    out_ref,
    pick_ref,
    attended_ref,
    normed_rel_ref,
    *refs,
):
    payload_refs = refs[:-5]
    d_mixed_ref, d_attended_ref, gates_ref, keep_ref, send_ref = refs[-5:]
    row_count, width = mixed_ref.shape
    experts, capacity = payload_refs[0].shape[0], payload_refs[0].shape[1] - TAIL
    first_slots, second_slots = slots_ref[:, 0:1], slots_ref[:, 1:2]
    first_grad = jnp.zeros((row_count, 1), jnp.float32)
    second_grad = jnp.zeros((row_count, 1), jnp.float32)
    d_normed = jnp.zeros((row_count, width), jnp.float32)
    for part, payload_ref in enumerate(payload_refs):
        places = places_ref[part : part + 1, :]
        select = jnp.where((places == first_slots) | (places == second_slots), 1.0, 0.0)
        rows = payload_ref[...].reshape(experts * (capacity + TAIL), width)
        d_normed += times(select.astype(jnp.bfloat16), rows)
        for expert in range(experts):
            first_place = (expert * len(payload_refs) + part) * capacity
            place = first_place + lax.broadcasted_iota(jnp.int32, (row_count, capacity), 1)
            tail = payload_ref[expert, capacity:, :capacity].astype(jnp.float32)
            d_gate = tail[0:1, :] + tail[1:2, :]
            first_grad += jnp.sum(
                jnp.where(place == first_slots, d_gate, 0.0), axis=1, keepdims=True
            )
            second_grad += jnp.sum(
                jnp.where(place == second_slots, d_gate, 0.0), axis=1, keepdims=True
            )
    logits = times(normed_ref[...], router_ref[...])
    first_ids, second_ids = experts_ref[:, 0:1], experts_ref[:, 1:2]
    first_gate, second_gate = two_gates(logits, first_ids, second_ids)
    mean = first_gate * first_grad + second_gate * second_grad
    column = lax.broadcasted_iota(jnp.int32, logits.shape, 1)
    d_logits = jnp.where(
        column == first_ids,
        first_gate * (first_grad - mean),
        jnp.where(column == second_ids, second_gate * (second_grad - mean), 0.0),
    ).astype(jnp.bfloat16)
    gates_ref[:, 0:1] = first_gate
    gates_ref[:, 1:2] = second_gate
    d_normed = d_normed + times_trans(d_logits, router_ref[...])
    mixed = mixed_ref[...]
    inverse = lax.rsqrt(jnp.mean(mixed * mixed, axis=1, keepdims=True) + EPSILON)
    d_gain = jnp.sum(d_normed * mixed * inverse, axis=0, keepdims=True)
    scaled = d_normed * gain_ref[...]
    pulled = jnp.mean(scaled * mixed, axis=1, keepdims=True) * inverse * inverse
    d_mixed = cotangent_ref[...].astype(jnp.float32) + inverse * (scaled - mixed * pulled)
    d_mixed_ref[...] = d_mixed
    d_branch = d_mixed.astype(jnp.bfloat16)
    d_attended_ref[...] = times_trans(d_branch, out_ref[...]).astype(jnp.bfloat16)
    small = trans_times(normed_rel_ref[...], d_logits)
    column = lax.broadcasted_iota(jnp.int32, small.shape, 1)
    gain_column = jnp.sum(
        pick_ref[...].astype(jnp.float32) * d_gain, axis=1, keepdims=True
    )
    small = jnp.where(column == small.shape[1] - 1, gain_column, small)
    half = width // 2
    keep_ref[:, width:] = small[:half]
    send_ref[:, width:] = small[half:].astype(jnp.bfloat16)
    keep_ref[:, :width] = trans_times(attended_ref[:, :half], d_branch)
    send_ref[:, :width] = trans_times(attended_ref[:, half:], d_branch).astype(jnp.bfloat16)


def collect(
    slots,
    experts,
    normed,
    mixed,
    cotangent,
    router,
    gain,
    weight_out,
    pick,
    attended_rel,
    normed_rel,
    payloads,
):
    row_count, width = mixed.shape
    sources, tall, _ = payloads[0].shape
    inside = jnp.arange(tall, dtype=jnp.int32)
    places = jnp.stack(
        [
            jnp.where(
                inside[None, :] < tall - TAIL,
                (jnp.arange(sources, dtype=jnp.int32)[:, None] * len(payloads) + part)
                * (tall - TAIL)
                + inside[None, :],
                -1,
            ).reshape(-1)
            for part in range(len(payloads))
        ]
    )
    columns = width + router.shape[1]
    return pl.pallas_call(
        collect_kernel,
        out_shape=(
            jax.ShapeDtypeStruct((row_count, width), jnp.float32),
            jax.ShapeDtypeStruct((row_count, width), jnp.bfloat16),
            jax.ShapeDtypeStruct((row_count, 2), jnp.float32),
            jax.ShapeDtypeStruct((width // 2, columns), jnp.float32),
            jax.ShapeDtypeStruct((width // 2, columns), jnp.bfloat16),
        ),
        compiler_params=pltpu.CompilerParams(vmem_limit_bytes=VMEM_BYTES),
        cost_estimate=pl.CostEstimate(flops=1000, bytes_accessed=1000, transcendentals=0),
        name="collect",
    )(
        slots,
        experts,
        places,
        normed,
        mixed,
        cotangent,
        router,
        gain,
        weight_out,
        pick,
        attended_rel,
        normed_rel,
        *payloads,
    )


def finish_kernel(slots_ref, gates_ref, mixed_ref, produced_ref, output_ref):
    row_count, width = mixed_ref.shape
    experts, capacity, _ = produced_ref.shape
    produced = produced_ref[...].reshape(experts * capacity, width)
    place = lax.broadcasted_iota(jnp.int32, (row_count, experts * capacity), 1)
    total = mixed_ref[...]
    for which in range(2):
        select = jnp.where(place == slots_ref[:, which : which + 1], 1.0, 0.0)
        found = times(select.astype(jnp.bfloat16), produced)
        total = total + gates_ref[:, which : which + 1] * found
    output_ref[...] = total.astype(jnp.bfloat16)


def finish(slots, gates, mixed, produced):
    row_count, width = mixed.shape
    return pl.pallas_call(
        finish_kernel,
        out_shape=jax.ShapeDtypeStruct((row_count, width), jnp.bfloat16),
        compiler_params=pltpu.CompilerParams(vmem_limit_bytes=VMEM_BYTES),
        cost_estimate=pl.CostEstimate(flops=1000, bytes_accessed=1000, transcendentals=0),
        name="finish",
    )(slots, gates, mixed, produced)


def slot_position(device_ids, experts):
    flat_ids = device_ids.reshape(-1)
    chosen = (flat_ids[:, None] == jnp.arange(experts, dtype=jnp.int32)[None, :]).astype(jnp.int32)
    before = jnp.cumsum(chosen, axis=0, dtype=jnp.int32) - chosen
    position = jnp.sum(before * chosen, axis=1, dtype=jnp.int32)
    return position.reshape(device_ids.shape)


def swap(rows, axis, size, step):
    return lax.ppermute(rows, axis, [(index, index ^ step) for index in range(size)])


def after(values, *earlier):
    return lax.optimization_barrier((values,) + earlier)[0]


def trade(blocks):
    return lax.all_to_all(blocks, "fsdp", split_axis=0, concat_axis=0, tiled=True)


class Ring:
    def __init__(self, fsdp, rep, own_rows):
        self.fsdp, self.rep, self.own_rows = fsdp, rep, own_rows
        self.relative = fsdp == 8 and rep == 4
        self.half = own_rows * fsdp * rep // 2

    def order(self, which):
        row = jnp.arange(self.half, dtype=jnp.int32)
        if not self.relative:
            return row + which * self.half
        group = row // self.own_rows
        mask = which + 8 * (group & 1) + 16 * ((group >> 1) & 1) + 2 * ((group >> 2) & 1)
        mask = mask + 4 * ((group >> 3) & 1)
        device = lax.axis_index("fsdp") * self.rep + lax.axis_index("rep")
        return (device ^ mask) * self.own_rows + row % self.own_rows

    def hop(self, rows, bit):
        return swap(rows, "rep", 4, bit) if bit < 4 else swap(rows, "fsdp", 8, bit // 4)

    def line(self, shard):
        if not self.relative:
            return shard
        return jnp.concatenate([shard] + [self.hop(shard, bit) for bit in (8, 16, 24)])

    def gather(self, line, cut):
        if not self.relative:
            whole = lax.all_gather(line, ("fsdp", "rep"), axis=0, tiled=True)
            halves = (whole[: self.half], whole[self.half :])
            return tuple(h[:, :cut] for h in halves), tuple(h[:, cut:] for h in halves)
        parts = []
        for columns, early, late in ((line[:, :cut], 2, 4), (line[:, cut:], 4, 2)):
            one = self.hop(columns, early)
            two = self.hop(columns, late)
            both = self.hop(one, late)
            by_y, by_x = (one, two) if early == 2 else (two, one)
            parts.append(jnp.concatenate([columns, by_y, by_x, both]))
        return tuple((part, self.hop(part, 1)) for part in parts)

    def group(self, rows):
        if not self.relative:
            return lax.all_gather(rows, "fsdp", axis=0)
        rows = rows[None]
        for bit in (4, 8, 16):
            rows = jnp.concatenate([rows, self.hop(rows, bit)])
        return rows

    def by_source(self, rows):
        if not self.relative:
            return rows
        order = lax.axis_index("fsdp") ^ jnp.arange(self.fsdp, dtype=jnp.int32)
        return jnp.take(rows, order, axis=0)

    def scatter(self, keep, send, earlier):
        if not self.relative:
            whole = jnp.concatenate([keep, send.astype(jnp.float32)])
            return lax.psum_scatter(whole, ("fsdp", "rep"), scatter_dimension=0, tiled=True)
        low = jnp.bfloat16
        total = keep + self.hop(send, 1).astype(jnp.float32)
        cut = -(-total.shape[1] // 256) * 128
        results = []
        quarter = self.half // 4
        for columns, first in ((total[:, :cut], 4), (total[:, cut:], 2)):
            if first == 4:
                kept, sent = columns[: 2 * quarter], columns[2 * quarter :]
            else:
                kept = jnp.concatenate([columns[:quarter], columns[2 * quarter : 3 * quarter]])
                sent = jnp.concatenate([columns[quarter : 2 * quarter], columns[3 * quarter :]])
            columns = kept + self.hop(sent.astype(low), first).astype(jnp.float32)
            for bit in (6 - first, 16, 8):
                if bit == 16:
                    columns = after(columns, earlier)
                middle = columns.shape[0] // 2
                got = self.hop(columns[middle:].astype(low), bit)
                columns = columns[:middle] + got.astype(jnp.float32)
            results.append(columns)
        return jnp.concatenate(results, axis=1)

    def total(self, values, earlier):
        if not self.relative:
            return lax.psum(values, ("fsdp", "rep"))
        for bit in (1, 2, 4, 8, 16):
            if bit == 8:
                values = after(values, earlier)
            values = values + self.hop(values, bit)
        return values

    def own(self, values):
        device = lax.axis_index("fsdp") * self.rep + lax.axis_index("rep")
        return lax.dynamic_slice_in_dim(values, device * self.own_rows, self.own_rows, 0)


def scatter_rep(piece_of, size):
    me = lax.axis_index("rep")
    low = jnp.bfloat16
    far_near = swap(piece_of(me ^ 3).astype(low), "rep", size, 1)
    near = swap(piece_of(me ^ 1).astype(low), "rep", size, 1)
    far = (piece_of(me ^ 2) + far_near.astype(jnp.float32)).astype(low)
    far = swap(far, "rep", size, 2)
    return piece_of(me) + near.astype(jnp.float32), far


def add_late(near_sum, far, earlier):
    near_sum, far = lax.optimization_barrier((near_sum, far, earlier))[:2]
    return near_sum + far.astype(jnp.float32)


def shards(
    fsdp,
    rep,
    tokens,
    attn_gain,
    qkv_weight,
    out_weight,
    ffn_gain,
    router_weight,
    expert_in,
    expert_out,
    bias_table,
    seq_lengths,
    bucket_map,
    expert_ids,
    cotangent,
):
    row_count, model_width = tokens.shape
    head_count, buckets = bias_table.shape
    head_size = model_width // head_count
    experts = router_weight.shape[1]
    capacity = 4 * row_count // experts
    highest = lax.Precision.HIGHEST
    own_rows, qkv_width = qkv_weight.shape
    extra = -(-(experts + 2) // LANES) * LANES
    me = lax.axis_index("fsdp")
    ring = Ring(fsdp, rep, own_rows)
    cut = qkv_width // 2

    small = jnp.concatenate(
        [
            router_weight,
            attn_gain[:, None],
            ffn_gain[:, None],
            jnp.zeros((own_rows, extra - experts - 2), jnp.bfloat16),
        ],
        axis=1,
    )
    line_qkv = ring.line(jnp.concatenate([qkv_weight, small], axis=1))
    first, second = ring.gather(line_qkv, cut)
    weight_out = lax.all_gather(out_weight, ("fsdp", "rep"), axis=0, tiled=True)

    position = slot_position(expert_ids, experts)
    slot_ids = expert_ids * capacity + position
    group_ids = ring.group(expert_ids)
    to_me = group_ids == me
    named = jnp.any(to_me, axis=2)
    other_ids = jnp.where(to_me[:, :, 0], group_ids[:, :, 1], group_ids[:, :, 0])
    places = jnp.where(named, jnp.cumsum(named, axis=1, dtype=jnp.int32) - 1, -1)
    slot_others = jnp.sum(
        jnp.where(
            places[:, None, :] == jnp.arange(capacity, dtype=jnp.int32)[None, :, None],
            other_ids[:, None, :],
            0,
        ),
        axis=2,
    )
    slot_others = ring.by_source(slot_others)
    slot_ids_across = slot_ids.T

    feature = jnp.arange(model_width, dtype=jnp.int32)
    picks = [
        (ring.order(which)[:, None] == feature[None, :]).astype(jnp.bfloat16) for which in range(2)
    ]
    pick = jnp.concatenate(picks)
    tokens_rel = times_trans(tokens, pick).astype(jnp.bfloat16)
    onehot = distance_onehot(bucket_map, row_count, buckets)
    base = lax.dot_general(bias_table, onehot, (((1,), (1,)), ((), ())), precision=highest)
    starts = sequence_starts(seq_lengths[0], row_count)

    sent_dy = spread(slot_ids_across, cotangent, experts, capacity)
    slot_dy = trade(after(sent_dy, line_qkv))
    weight_in = lax.all_gather(expert_in, "rep", axis=1, tiled=True)[0]
    weight_back = lax.all_gather(expert_out, "rep", axis=1, tiled=True)[0]

    def natural(halves):
        joined = trans_times(pick, jnp.concatenate(halves))
        return joined.astype(jnp.bfloat16)

    packed, *normed_halves = project(tokens_rel, first, second, experts, qkv_width)
    small = natural([half[:, qkv_width - cut :] for half in second])
    gains = small.T.astype(jnp.float32)
    gain_one, gain_two = gains[experts : experts + 1], gains[experts + 1 : experts + 2]
    attended = attention(base, starts, packed, head_size)
    mixed, normed_two, *sending = mix(
        slot_ids_across, tokens, attended, weight_out, gain_two, experts, capacity
    )
    place = me[None].astype(jnp.int32)
    size = capacity // PARTS
    arrived = [trade(after(sending[0], slot_dy))]
    arrived.append(trade(after(sending[1], arrived[0])))
    payloads, kept = [], None
    for part in range(PARTS):
        payload, kept = expert_rows(
            place,
            part,
            arrived[part],
            slot_dy,
            slot_others[:, part * size : (part + 1) * size].reshape(-1, 1),
            small,
            weight_in,
            weight_back,
            kept,
        )
        payloads.append(payload)
    produced, rows_all, slot_grad, active, d_hidden = kept
    payloads[0] = trade(payloads[0])
    payloads[1] = trade(after(payloads[1], payloads[0]))
    rows_all, slot_grad, active, d_hidden = lax.optimization_barrier(
        (rows_all, slot_grad, active, d_hidden, payloads[0])
    )[:4]
    returned = trade(after(produced, payloads[1]))

    in_rows = expert_in.shape[1]
    out_rows = expert_out.shape[1]
    owned_in = scatter_rep(
        lambda who: trans_times(
            lax.dynamic_slice_in_dim(rows_all, who * in_rows, in_rows, 1), d_hidden
        ),
        rep,
    )
    owned_out = scatter_rep(
        lambda who: trans_times(
            lax.dynamic_slice_in_dim(active, who * out_rows, out_rows, 1), slot_grad
        ),
        rep,
    )

    attended_rel = times_trans(attended, pick).astype(jnp.bfloat16)
    normed_rel = times_trans(normed_two, pick).astype(jnp.bfloat16)
    d_mixed, d_attended, gates, *out_pieces = collect(
        slot_ids,
        expert_ids,
        normed_two,
        mixed,
        cotangent,
        small,
        gain_two,
        weight_out,
        pick,
        attended_rel,
        normed_rel,
        payloads,
    )
    owned_out_weight = ring.scatter(*out_pieces, returned)
    early = owned_out_weight[:, model_width:]
    d_packed, d_base, *qkv_pieces = attention_pull(
        base, starts, packed, d_attended, normed_halves, head_size
    )
    owned_qkv = ring.scatter(*qkv_pieces, returned)
    weight_qkv = jnp.concatenate(
        [natural(first), natural([half[:, : qkv_width - cut] for half in second])], axis=1
    )
    d_normed_one = times_trans(d_packed, weight_qkv)
    inputs = tokens.astype(jnp.float32)
    unused_one, norm_pull_one = jax.vjp(rms_norm, inputs, gain_one)
    d_inputs_norm, d_gain_one = norm_pull_one(d_normed_one)
    token_grad = d_mixed + d_inputs_norm
    bias_local = jnp.dot(d_base, onehot, precision=highest)
    late = jnp.concatenate([d_gain_one.reshape(-1), bias_local.reshape(-1)])
    late = ring.total(late, returned)
    output = finish(slot_ids, gates, mixed, returned)
    return (
        output,
        token_grad,
        ring.own(late[:model_width]),
        owned_qkv,
        owned_out_weight[:, :model_width],
        early[:, -1],
        early[:, :experts],
        add_late(*owned_in, d_packed)[None],
        add_late(*owned_out, d_packed)[None],
        late[model_width:].reshape(bias_table.shape),
    )


def solution(mesh):
    return jax.shard_map(
        functools.partial(shards, mesh.shape["fsdp"], mesh.shape["rep"]),
        mesh=mesh,
        in_specs=(
            P(("fsdp", "rep"), None),
            P(("fsdp", "rep")),
            P(("fsdp", "rep"), None),
            P(("fsdp", "rep"), None),
            P(("fsdp", "rep")),
            P(("fsdp", "rep"), None),
            P("fsdp", "rep", None),
            P("fsdp", "rep", None),
            P(),
            P(("fsdp", "rep"), None),
            P(),
            P(("fsdp", "rep"), None),
            P(("fsdp", "rep"), None),
        ),
        out_specs=(
            P(("fsdp", "rep"), None),
            P(("fsdp", "rep"), None),
            P(("fsdp", "rep")),
            P(("fsdp", "rep"), None),
            P(("fsdp", "rep"), None),
            P(("fsdp", "rep")),
            P(("fsdp", "rep"), None),
            P("fsdp", "rep", None),
            P("fsdp", "rep", None),
            P(),
        ),
        check_vma=False,
    )
```

```python
import functools

import jax
import jax.numpy as jnp
from jax import lax
from jax.experimental import pallas as pl
from jax.experimental.pallas import tpu as pltpu
from jax.sharding import PartitionSpec as P

EPSILON = 1e-06
MASKED = -1e30
GELU_COEF = 0.7978845608028654
TILE = 128
LANES = 128
PARTS = 2
TAIL = 16
VMEM_BYTES = 56 * 1024 * 1024


def rms_norm(values, gain_vector):
    return (
        values
        * lax.rsqrt(jnp.mean(values * values, axis=-1, keepdims=True) + EPSILON)
        * gain_vector
    )


def times(left_side, right_side):
    return lax.dot_general(
        left_side, right_side, (((1,), (0,)), ((), ())), preferred_element_type=jnp.float32
    )


def times_trans(left_side, right_side):
    return lax.dot_general(
        left_side, right_side, (((1,), (1,)), ((), ())), preferred_element_type=jnp.float32
    )


def trans_times(left_side, right_side):
    return lax.dot_general(
        left_side, right_side, (((0,), (0,)), ((), ())), preferred_element_type=jnp.float32
    )


def sequence_starts(lengths, row_count):
    seq_ends = jnp.cumsum(lengths, dtype=jnp.int32)
    places = jnp.arange(row_count, dtype=jnp.int32)
    passed = places[:, None] >= seq_ends[None, :]
    return jnp.max(jnp.where(passed, seq_ends[None, :], 0), axis=1, keepdims=True)


def distance_onehot(bucket_map, row_count, buckets):
    longest = bucket_map.shape[0]
    distance = row_count - TILE - jnp.arange(row_count, dtype=jnp.int32)
    place = jnp.arange(longest, dtype=jnp.int32)
    at_distance = jnp.sum(
        jnp.where(distance[:, None] == place[None, :], bucket_map[None, :] + 1, 0), axis=1
    )
    return (at_distance[:, None] == 1 + jnp.arange(buckets, dtype=jnp.int32)[None, :]).astype(
        jnp.float32
    )


def head_lanes(block, which, head_size):
    lane = lax.broadcasted_iota(jnp.int32, block.shape, 1)
    inside = (lane >= which * head_size) & (lane < (which + 1) * head_size)
    return jnp.where(inside, block, jnp.zeros_like(block))


def bias_strip(base_ref, head, row_count):
    row = base_ref[pl.ds(head, 1), :]
    spread = jnp.broadcast_to(row, (TILE, row_count))
    return pltpu.roll(spread, 0, 1, stride=1, stride_axis=0)


def tile_score(query_tile, keys, strip, starts, tile, scale):
    row_count = strip.shape[1]
    width = TILE * (tile + 1)
    score = times_trans(query_tile, keys[:width]) * scale + strip[:, row_count - width :]
    place = lax.broadcasted_iota(jnp.int32, score.shape, 1)
    row = lax.broadcasted_iota(jnp.int32, score.shape, 0) + TILE * tile
    return jnp.where((place <= row) & (place >= starts), score, MASKED)


def lane_block(first):
    return pl.ds(pl.multiple_of(first, LANES), LANES)


def attention_kernel(head_size, base_ref, starts_ref, packed_ref, attended_ref, level_ref):
    row_count, width = attended_ref.shape
    per_block = LANES // head_size
    scale = head_size ** (-0.5)

    @pl.loop(0, width // LANES)
    def _(block):
        queries = packed_ref[:, lane_block(block * LANES)]
        keys = packed_ref[:, lane_block(width + block * LANES)]
        values = packed_ref[:, lane_block(2 * width + block * LANES)]
        strips = [bias_strip(base_ref, block * per_block + own, row_count) for own in range(per_block)]
        for tile in range(row_count // TILE):
            rows = slice(tile * TILE, (tile + 1) * TILE)
            starts = starts_ref[rows, :]
            total = jnp.zeros((TILE, LANES), jnp.float32)
            for own in range(per_block):
                score = tile_score(
                    head_lanes(queries[rows], own, head_size), keys, strips[own], starts, tile, scale
                )
                peak = jnp.max(score, axis=1, keepdims=True)
                exponent = jnp.exp(score - peak)
                whole = jnp.sum(exponent, axis=1, keepdims=True)
                level_ref[block, rows, own : own + 1] = peak + jnp.log(whole)
                probs = (exponent * (1.0 / whole)).astype(jnp.bfloat16)
                total += times(probs, head_lanes(values[: probs.shape[1]], own, head_size))
            attended_ref[rows, lane_block(block * LANES)] = total.astype(jnp.bfloat16)


def attention(base, starts, packed, head_size):
    row_count = packed.shape[0]
    width = packed.shape[1] // 3
    return pl.pallas_call(
        functools.partial(attention_kernel, head_size),
        out_shape=(
            jax.ShapeDtypeStruct((row_count, width), jnp.bfloat16),
            jax.ShapeDtypeStruct((width // LANES, row_count, LANES // head_size), jnp.float32),
        ),
        compiler_params=pltpu.CompilerParams(vmem_limit_bytes=VMEM_BYTES),
        cost_estimate=pl.CostEstimate(flops=1000, bytes_accessed=1000, transcendentals=0),
        name="attention",
    )(base, starts, packed)


def attention_pull_kernel(
    head_size,
    base_ref,
    starts_ref,
    packed_ref,
    grad_ref,
    level_ref,
    kept_rows_ref,
    sent_rows_ref,
    out_keep_ref,
    out_send_ref,
    d_packed_ref,
    d_base_ref,
    keep_ref,
    send_ref,
    d_keys_ref,
    d_values_ref,
    d_strip_ref,
):
    row_count, width = grad_ref.shape
    per_block = LANES // head_size
    scale = head_size ** (-0.5)

    @pl.loop(0, width // LANES)
    def _(block):
        queries = packed_ref[:, lane_block(block * LANES)]
        keys = packed_ref[:, lane_block(width + block * LANES)]
        values = packed_ref[:, lane_block(2 * width + block * LANES)]
        grads = grad_ref[:, lane_block(block * LANES)]
        strips = [bias_strip(base_ref, block * per_block + own, row_count) for own in range(per_block)]
        d_keys_ref[...] = jnp.zeros_like(d_keys_ref)
        d_values_ref[...] = jnp.zeros_like(d_values_ref)
        d_strip_ref[...] = jnp.zeros_like(d_strip_ref)
        for tile in range(row_count // TILE):
            rows = slice(tile * TILE, (tile + 1) * TILE)
            reach = TILE * (tile + 1)
            starts = starts_ref[rows, :]
            d_queries = jnp.zeros((TILE, LANES), jnp.float32)
            for own in range(per_block):
                own_queries = head_lanes(queries[rows], own, head_size)
                own_grads = head_lanes(grads[rows], own, head_size)
                score = tile_score(own_queries, keys, strips[own], starts, tile, scale)
                probs = jnp.exp(score - level_ref[block, rows, own : own + 1])
                d_probs = times_trans(own_grads, values[:reach])
                row_delta = jnp.sum(probs * d_probs, axis=1, keepdims=True)
                d_score = (probs * (d_probs - row_delta)).astype(jnp.bfloat16)
                d_strip_ref[own, :, row_count - reach :] += d_score.astype(jnp.float32)
                d_queries += times(d_score, head_lanes(keys[:reach], own, head_size))
                d_keys_ref[:reach, :] += trans_times(d_score, own_queries)
                d_values_ref[:reach, :] += trans_times(probs.astype(jnp.bfloat16), own_grads)
            d_packed_ref[rows, lane_block(block * LANES)] = (d_queries * scale).astype(jnp.bfloat16)
        d_packed_ref[:, lane_block(width + block * LANES)] = (d_keys_ref[...] * scale).astype(
            jnp.bfloat16
        )
        d_packed_ref[:, lane_block(2 * width + block * LANES)] = d_values_ref[...].astype(
            jnp.bfloat16
        )
        for own in range(per_block):
            folded = d_strip_ref[own]
            half = TILE // 2
            while half >= 8:
                folded = folded[:half] + pltpu.roll(folded[half:], row_count - half, 1)
                half //= 2
            row = lax.broadcasted_iota(jnp.int32, folded.shape, 0)
            for bit in (4, 2, 1):
                folded = jnp.where(
                    (row & bit) != 0, pltpu.roll(folded, row_count - bit, 1), folded
                )
            d_base_ref[pl.ds(block * per_block + own, 1), :] = jnp.sum(
                folded, axis=0, keepdims=True
            )

    keep_ref[:, 3 * width :] = out_keep_ref[...]
    send_ref[:, 3 * width :] = out_send_ref[...]
    for start in range(0, 3 * width, width):
        columns = slice(start, start + width)
        send_ref[:, columns] = trans_times(sent_rows_ref[...], d_packed_ref[:, columns]).astype(
            jnp.bfloat16
        )
        keep_ref[:, columns] = trans_times(kept_rows_ref[...], d_packed_ref[:, columns])


def attention_pull(base, starts, packed, grads, levels, rows, out_pieces, head_size):
    row_count = grads.shape[0]
    half = rows[0].shape[1]
    columns = packed.shape[1] + out_pieces[0].shape[1]
    shape = jax.ShapeDtypeStruct
    return pl.pallas_call(
        functools.partial(attention_pull_kernel, head_size),
        out_shape=(
            shape(packed.shape, jnp.bfloat16),
            shape(base.shape, jnp.float32),
            shape((half, columns), jnp.float32),
            shape((half, columns), jnp.bfloat16),
        ),
        scratch_shapes=[
            pltpu.VMEM((row_count, LANES), jnp.float32),
            pltpu.VMEM((row_count, LANES), jnp.float32),
            pltpu.VMEM((LANES // head_size, TILE, row_count), jnp.float32),
        ],
        compiler_params=pltpu.CompilerParams(vmem_limit_bytes=VMEM_BYTES),
        cost_estimate=pl.CostEstimate(flops=1000, bytes_accessed=1000, transcendentals=0),
        name="attention_pull",
    )(base, starts, packed, grads, levels, *rows, *out_pieces)


def gelu_parts(values):
    inner = GELU_COEF * (values + 0.044715 * values * values * values)
    bend = jnp.tanh(inner)
    slope = 0.5 * (1.0 + bend) + 0.5 * values * (1.0 - bend * bend) * (
        GELU_COEF * (1.0 + 3.0 * 0.044715 * values * values)
    )
    return 0.5 * values * (1.0 + bend), slope


def vmem():
    return pl.BlockSpec(memory_space=pltpu.VMEM)


def two_gates(logits, first_ids, second_ids):
    column = lax.broadcasted_iota(jnp.int32, logits.shape, 1)
    first = jnp.sum(jnp.where(column == first_ids, logits, 0.0), axis=1, keepdims=True)
    second = jnp.sum(jnp.where(column == second_ids, logits, 0.0), axis=1, keepdims=True)
    peak = jnp.maximum(first, second)
    first, second = jnp.exp(first - peak), jnp.exp(second - peak)
    return first / (first + second), second / (first + second)


def project_kernel(column, tokens_ref, *refs):
    first_refs, second_refs = refs[0:2], refs[2:4]
    packed_ref, normed_refs = refs[4], refs[5:7]
    row_count, half = normed_refs[0].shape
    cut = first_refs[0].shape[1]
    rest = packed_ref.shape[1] - cut
    inputs = tokens_ref[...].astype(jnp.float32)
    inverse = lax.rsqrt(jnp.mean(inputs * inputs, axis=1, keepdims=True) + EPSILON)
    for which in range(2):
        small = second_refs[which][:, rest:].astype(jnp.float32)
        gain = jnp.transpose(small)[column : column + 1, :]
        normed = (inputs[:, which * half : (which + 1) * half] * inverse * gain).astype(
            jnp.bfloat16
        )
        normed_refs[which][...] = normed
    both = jnp.concatenate([normed_refs[0][...], normed_refs[1][...]], axis=1)
    for refs_of, start, width in ((first_refs, 0, cut), (second_refs, cut, rest)):
        weights = jnp.concatenate([refs_of[0][:, :width], refs_of[1][:, :width]], axis=0)
        packed_ref[:, start : start + width] = times(both, weights).astype(jnp.bfloat16)


def project(tokens_rel, first, second, column, qkv_width):
    row_count, width = tokens_rel.shape
    half = jax.ShapeDtypeStruct((row_count, width // 2), jnp.bfloat16)
    return pl.pallas_call(
        functools.partial(project_kernel, column),
        out_shape=(jax.ShapeDtypeStruct((row_count, qkv_width), jnp.bfloat16), half, half),
        compiler_params=pltpu.CompilerParams(vmem_limit_bytes=VMEM_BYTES),
        cost_estimate=pl.CostEstimate(flops=1000, bytes_accessed=1000, transcendentals=0),
        name="project",
    )(tokens_rel, *first, *second)


def slot_rows_of(ids_ref, rows, first_place, count):
    place = first_place + lax.broadcasted_iota(jnp.int32, (count, rows.shape[0]), 0)
    inside = (place == ids_ref[0:1, :]) | (place == ids_ref[1:2, :])
    return times(jnp.where(inside, 1.0, 0.0).astype(jnp.bfloat16), rows).astype(jnp.bfloat16)


def fill_blocks(ids_ref, rows, block_refs):
    experts, count, _ = block_refs[0].shape
    for part, block_ref in enumerate(block_refs):
        for expert in range(experts):
            place = (expert * len(block_refs) + part) * count
            block_ref[expert] = slot_rows_of(ids_ref, rows, place, count)


def spread_kernel(ids_ref, rows_ref, block_ref):
    fill_blocks(ids_ref, rows_ref[...], [block_ref])


def spread(slot_ids, rows, experts, capacity):
    row_count, width = rows.shape
    return pl.pallas_call(
        spread_kernel,
        out_shape=jax.ShapeDtypeStruct((experts, capacity, width), jnp.bfloat16),
        compiler_params=pltpu.CompilerParams(vmem_limit_bytes=VMEM_BYTES),
        cost_estimate=pl.CostEstimate(flops=1000, bytes_accessed=1000, transcendentals=0),
        name="spread",
    )(slot_ids, rows)


def mix_kernel(
    ids_ref, tokens_ref, attended_ref, out_ref, gain_ref, mixed_ref, normed_ref, *block_refs
):
    mixed = tokens_ref[...].astype(jnp.float32) + times(attended_ref[...], out_ref[...])
    mixed_ref[...] = mixed
    inverse = lax.rsqrt(jnp.mean(mixed * mixed, axis=1, keepdims=True) + EPSILON)
    normed_ref[...] = (mixed * inverse * gain_ref[...]).astype(jnp.bfloat16)
    fill_blocks(ids_ref, normed_ref[...], block_refs)


def mix(slot_ids, tokens, attended, weight_out, gain, experts, capacity):
    row_count, width = tokens.shape
    block = jax.ShapeDtypeStruct((experts, capacity // PARTS, width), jnp.bfloat16)
    return pl.pallas_call(
        mix_kernel,
        out_shape=(
            jax.ShapeDtypeStruct((row_count, width), jnp.float32),
            jax.ShapeDtypeStruct((row_count, width), jnp.bfloat16),
        )
        + (block,) * PARTS,
        compiler_params=pltpu.CompilerParams(vmem_limit_bytes=VMEM_BYTES),
        cost_estimate=pl.CostEstimate(flops=1000, bytes_accessed=1000, transcendentals=0),
        name="mix",
    )(slot_ids, tokens, attended, weight_out, gain)


def expert_kernel(
    part,
    place_ref,
    rows_ref,
    grads_ref,
    other_ref,
    router_ref,
    in_ref,
    out_ref,
    *refs,
):
    payload_ref, produced_ref, rows_all, slot_grad_all, active_ref, d_hidden_ref = refs[-11:-5]
    tails_ref = refs[-5] if part == 0 else refs[0]
    rows, slot_grad, produced_sum, row_sum = refs[-4:]
    sources, capacity, width = rows_ref.shape
    count = sources * capacity
    step = pl.program_id(0)

    @pl.when(step == 0)
    def _():
        rows[...] = rows_ref[...].reshape(count, width)
        logits = times(rows[...], router_ref[...])
        own_ids = jnp.full((count, 1), place_ref[0], jnp.int32)
        gate, unused_gate = two_gates(logits, own_ids, other_ref[...])
        grads = grads_ref[...].reshape(count, width).astype(jnp.float32)
        slot_grad[...] = (gate * grads).astype(jnp.bfloat16)
        rows_all[...] = rows[...]
        slot_grad_all[...] = slot_grad[...]
        produced_sum[...] = jnp.zeros_like(produced_sum)
        row_sum[...] = jnp.zeros_like(row_sum)

    hidden = times(rows[...], in_ref[...])
    active, slope = gelu_parts(hidden)
    active = active.astype(jnp.bfloat16)
    active_ref[...] = active
    d_active = times_trans(slot_grad[...], out_ref[...])
    d_hidden = (slope * d_active).astype(jnp.bfloat16)
    d_hidden_ref[...] = d_hidden
    produced_sum[...] += times(active, out_ref[...])
    row_sum[...] += times_trans(d_hidden, in_ref[...])

    @pl.when(step == pl.num_programs(0) - 1)
    def _():
        for source in range(sources):
            own = slice(source * capacity, (source + 1) * capacity)
            result = produced_sum[own, :].astype(jnp.bfloat16)
            produced_ref[source] = result
            payload_ref[source, :capacity, :] = row_sum[own, :].astype(jnp.bfloat16)
            d_gate = jnp.sum(
                result.astype(jnp.float32) * grads_ref[source].astype(jnp.float32),
                axis=1,
                keepdims=True,
            )
            across = jnp.transpose(jnp.broadcast_to(d_gate, (capacity, LANES)))[:TAIL, :]
            high = across.astype(jnp.bfloat16).astype(jnp.float32)
            row = lax.broadcasted_iota(jnp.int32, across.shape, 0) - 2 * part
            tail = jnp.where(row == 0, high, jnp.where(row == 1, across - high, 0.0))
            if part == 0:
                tails_ref[source, :, :] = tail
            else:
                tail = (tails_ref[source, :, :] + tail).astype(jnp.bfloat16)
                payload_ref[source, capacity:, :] = jnp.zeros((TAIL, width), jnp.bfloat16)
                payload_ref[source, capacity:, :capacity] = tail


def expert_rows(place, part, rows, grads, other, router, weight_in, weight_out, earlier):
    sources, capacity, width = rows.shape
    hidden_width = weight_in.shape[1]
    chunk = hidden_width // 4
    count = sources * capacity

    def whole(shape):
        return pl.BlockSpec(shape, lambda i, place: (0,) * len(shape))

    def part_of(*shape):
        return pl.BlockSpec(shape, lambda i, place: (0, part, 0))

    def part_block(columns):
        return pl.BlockSpec((count, columns), lambda i, place: (part, 0))

    def part_chunk():
        return pl.BlockSpec((count, chunk), lambda i, place: (part, i))

    def full(*shape):
        return jax.ShapeDtypeStruct(shape, jnp.bfloat16)

    total = PARTS * count
    operands = (rows, grads, other, router, weight_in, weight_out)
    in_specs = [
        whole(rows.shape),
        part_of(sources, capacity, width),
        whole(other.shape),
        whole(router.shape),
        pl.BlockSpec((width, chunk), lambda i, place: (0, i)),
        pl.BlockSpec((chunk, width), lambda i, place: (i, 0)),
    ]
    aliases = {}
    if earlier is not None:
        earlier, tails = earlier[:-1], earlier[-1]
        operands = operands + (tails,)
        in_specs = in_specs + [whole(tails.shape)]
        aliases = {1 + len(operands) + which: 1 + which for which in range(5)}
        operands = operands + tuple(earlier)
        in_specs = in_specs + [pl.BlockSpec(memory_space=pl.ANY)] * 5
    results = pl.pallas_call(
        functools.partial(expert_kernel, part),
        grid_spec=pltpu.PrefetchScalarGridSpec(
            num_scalar_prefetch=1,
            grid=(4,),
            in_specs=in_specs,
            out_specs=[
                whole((sources, capacity + part * TAIL, width)),
                part_of(sources, capacity, width),
                part_block(width),
                part_block(width),
                part_chunk(),
                part_chunk(),
                whole((sources, TAIL, capacity)),
            ],
            scratch_shapes=[
                pltpu.VMEM((count, width), jnp.bfloat16),
                pltpu.VMEM((count, width), jnp.bfloat16),
                pltpu.VMEM((count, width), jnp.float32),
                pltpu.VMEM((count, width), jnp.float32),
            ],
        ),
        out_shape=[
            full(sources, capacity + part * TAIL, width),
            full(sources, PARTS * capacity, width),
            full(total, width),
            full(total, width),
            full(total, hidden_width),
            full(total, hidden_width),
            jax.ShapeDtypeStruct((sources, TAIL, capacity), jnp.float32),
        ],
        input_output_aliases=aliases,
        compiler_params=pltpu.CompilerParams(vmem_limit_bytes=VMEM_BYTES),
        cost_estimate=pl.CostEstimate(
            flops=8 * count * width * hidden_width,
            bytes_accessed=4 * count * (hidden_width + 4 * width) + 4 * width * hidden_width,
            transcendentals=count * hidden_width,
        ),
        name="expert_rows",
    )(place, *operands)
    return results[0], results[1:]


def collect_kernel(
    slots_ref,
    experts_ref,
    places_ref,
    normed_ref,
    mixed_ref,
    cotangent_ref,
    router_ref,
    gain_ref,
    out_ref,
    pick_ref,
    attended_ref,
    normed_rel_ref,
    *refs,
):
    payload_refs = refs[:-5]
    d_mixed_ref, d_attended_ref, gates_ref, keep_ref, send_ref = refs[-5:]
    row_count, width = mixed_ref.shape
    experts, capacity, _ = payload_refs[0].shape
    first_slots, second_slots = slots_ref[:, 0:1], slots_ref[:, 1:2]
    first_grad = jnp.zeros((row_count, 1), jnp.float32)
    second_grad = jnp.zeros((row_count, 1), jnp.float32)
    d_normed = jnp.zeros((row_count, width), jnp.float32)
    for part, payload_ref in enumerate(payload_refs):
        places = places_ref[part : part + 1, :]
        select = jnp.where((places == first_slots) | (places == second_slots), 1.0, 0.0)
        d_normed += times(select.astype(jnp.bfloat16), payload_ref[:, :capacity, :].reshape(-1, width))
        for expert in range(experts):
            first_place = (expert * len(payload_refs) + part) * capacity
            place = first_place + lax.broadcasted_iota(jnp.int32, (row_count, capacity), 1)
            tail = payload_refs[-1][expert, capacity:, :capacity].astype(jnp.float32)
            d_gate = tail[2 * part : 2 * part + 1, :] + tail[2 * part + 1 : 2 * part + 2, :]
            first_grad += jnp.sum(
                jnp.where(place == first_slots, d_gate, 0.0), axis=1, keepdims=True
            )
            second_grad += jnp.sum(
                jnp.where(place == second_slots, d_gate, 0.0), axis=1, keepdims=True
            )
    logits = times(normed_ref[...], router_ref[...])
    first_ids, second_ids = experts_ref[:, 0:1], experts_ref[:, 1:2]
    first_gate, second_gate = two_gates(logits, first_ids, second_ids)
    mean = first_gate * first_grad + second_gate * second_grad
    column = lax.broadcasted_iota(jnp.int32, logits.shape, 1)
    d_logits = jnp.where(
        column == first_ids,
        first_gate * (first_grad - mean),
        jnp.where(column == second_ids, second_gate * (second_grad - mean), 0.0),
    ).astype(jnp.bfloat16)
    gates_ref[:, 0:1] = first_gate
    gates_ref[:, 1:2] = second_gate
    d_normed = d_normed + times_trans(d_logits, router_ref[...])
    mixed = mixed_ref[...]
    inverse = lax.rsqrt(jnp.mean(mixed * mixed, axis=1, keepdims=True) + EPSILON)
    d_gain = jnp.sum(d_normed * mixed * inverse, axis=0, keepdims=True)
    scaled = d_normed * gain_ref[...]
    pulled = jnp.mean(scaled * mixed, axis=1, keepdims=True) * inverse * inverse
    d_mixed = cotangent_ref[...].astype(jnp.float32) + inverse * (scaled - mixed * pulled)
    d_mixed_ref[...] = d_mixed
    d_branch = d_mixed.astype(jnp.bfloat16)
    d_attended_ref[...] = times_trans(d_branch, out_ref[...]).astype(jnp.bfloat16)
    small = trans_times(normed_rel_ref[...], d_logits)
    column = lax.broadcasted_iota(jnp.int32, small.shape, 1)
    gain_column = jnp.sum(
        pick_ref[...].astype(jnp.float32) * d_gain, axis=1, keepdims=True
    )
    small = jnp.where(column == small.shape[1] - 1, gain_column, small)
    half = width // 2
    keep_ref[:, width:] = small[:half]
    send_ref[:, width:] = small[half:].astype(jnp.bfloat16)
    keep_ref[:, :width] = trans_times(attended_ref[:, :half], d_branch)
    send_ref[:, :width] = trans_times(attended_ref[:, half:], d_branch).astype(jnp.bfloat16)


def collect(
    slots,
    experts,
    normed,
    mixed,
    cotangent,
    router,
    gain,
    weight_out,
    pick,
    attended_rel,
    normed_rel,
    payloads,
):
    row_count, width = mixed.shape
    sources, size, _ = payloads[0].shape
    places = (
        (jnp.arange(sources, dtype=jnp.int32)[None, :, None] * len(payloads)
        + jnp.arange(len(payloads), dtype=jnp.int32)[:, None, None])
        * size
        + jnp.arange(size, dtype=jnp.int32)[None, None, :]
    ).reshape(len(payloads), sources * size)
    columns = width + router.shape[1]
    return pl.pallas_call(
        collect_kernel,
        out_shape=(
            jax.ShapeDtypeStruct((row_count, width), jnp.float32),
            jax.ShapeDtypeStruct((row_count, width), jnp.bfloat16),
            jax.ShapeDtypeStruct((row_count, 2), jnp.float32),
            jax.ShapeDtypeStruct((width // 2, columns), jnp.float32),
            jax.ShapeDtypeStruct((width // 2, columns), jnp.bfloat16),
        ),
        compiler_params=pltpu.CompilerParams(vmem_limit_bytes=VMEM_BYTES),
        cost_estimate=pl.CostEstimate(flops=1000, bytes_accessed=1000, transcendentals=0),
        name="collect",
    )(
        slots,
        experts,
        places,
        normed,
        mixed,
        cotangent,
        router,
        gain,
        weight_out,
        pick,
        attended_rel,
        normed_rel,
        *payloads,
    )


def finish_kernel(slots_ref, gates_ref, mixed_ref, produced_ref, output_ref):
    row_count, width = mixed_ref.shape
    experts, capacity, _ = produced_ref.shape
    produced = produced_ref[...].reshape(experts * capacity, width)
    place = lax.broadcasted_iota(jnp.int32, (row_count, experts * capacity), 1)
    total = mixed_ref[...]
    for which in range(2):
        select = jnp.where(place == slots_ref[:, which : which + 1], 1.0, 0.0)
        found = times(select.astype(jnp.bfloat16), produced)
        total = total + gates_ref[:, which : which + 1] * found
    output_ref[...] = total.astype(jnp.bfloat16)


def finish(slots, gates, mixed, produced):
    row_count, width = mixed.shape
    return pl.pallas_call(
        finish_kernel,
        out_shape=jax.ShapeDtypeStruct((row_count, width), jnp.bfloat16),
        compiler_params=pltpu.CompilerParams(vmem_limit_bytes=VMEM_BYTES),
        cost_estimate=pl.CostEstimate(flops=1000, bytes_accessed=1000, transcendentals=0),
        name="finish",
    )(slots, gates, mixed, produced)


def slot_position(device_ids, experts):
    flat_ids = device_ids.reshape(-1)
    chosen = (flat_ids[:, None] == jnp.arange(experts, dtype=jnp.int32)[None, :]).astype(jnp.int32)
    before = jnp.cumsum(chosen, axis=0, dtype=jnp.int32) - chosen
    position = jnp.sum(before * chosen, axis=1, dtype=jnp.int32)
    return position.reshape(device_ids.shape)


def swap(rows, axis, size, step):
    return lax.ppermute(rows, axis, [(index, index ^ step) for index in range(size)])


def after(values, *earlier):
    return lax.optimization_barrier((values,) + earlier)[0]


def trade(blocks):
    return lax.all_to_all(blocks, "fsdp", split_axis=0, concat_axis=0, tiled=True)


class Ring:
    def __init__(self, fsdp, rep, own_rows):
        self.fsdp, self.rep, self.own_rows = fsdp, rep, own_rows
        self.relative = fsdp == 8 and rep == 4
        self.half = own_rows * fsdp * rep // 2

    def order(self, which):
        row = jnp.arange(self.half, dtype=jnp.int32)
        if not self.relative:
            return row + which * self.half
        group = row // self.own_rows
        mask = which + 8 * (group & 1) + 16 * ((group >> 1) & 1) + 2 * ((group >> 2) & 1)
        mask = mask + 4 * ((group >> 3) & 1)
        device = lax.axis_index("fsdp") * self.rep + lax.axis_index("rep")
        return (device ^ mask) * self.own_rows + row % self.own_rows

    def hop(self, rows, bit):
        return swap(rows, "rep", 4, bit) if bit < 4 else swap(rows, "fsdp", 8, bit // 4)

    def line(self, shard):
        if not self.relative:
            return shard
        return jnp.concatenate([shard] + [self.hop(shard, bit) for bit in (8, 16, 24)])

    def gather(self, line, cut):
        if not self.relative:
            whole = lax.all_gather(line, ("fsdp", "rep"), axis=0, tiled=True)
            halves = (whole[: self.half], whole[self.half :])
            return tuple(h[:, :cut] for h in halves), tuple(h[:, cut:] for h in halves)
        parts = []
        for columns, early, late in ((line[:, :cut], 2, 4), (line[:, cut:], 4, 2)):
            one = self.hop(columns, early)
            two = self.hop(columns, late)
            both = self.hop(one, late)
            by_y, by_x = (one, two) if early == 2 else (two, one)
            parts.append(jnp.concatenate([columns, by_y, by_x, both]))
        return tuple((part, self.hop(part, 1)) for part in parts)

    def group(self, rows):
        if not self.relative:
            return lax.all_gather(rows, "fsdp", axis=0)
        rows = rows[None]
        for bit in (4, 8, 16):
            rows = jnp.concatenate([rows, self.hop(rows, bit)])
        return rows

    def by_source(self, rows):
        if not self.relative:
            return rows
        order = lax.axis_index("fsdp") ^ jnp.arange(self.fsdp, dtype=jnp.int32)
        return jnp.take(rows, order, axis=0)

    def scatter(self, keep, send, earlier):
        if not self.relative:
            whole = jnp.concatenate([keep, send.astype(jnp.float32)])
            return lax.psum_scatter(whole, ("fsdp", "rep"), scatter_dimension=0, tiled=True)
        total = keep + self.hop(send, 1).astype(jnp.float32)
        low = jnp.bfloat16
        cut = -(-total.shape[1] // 256) * 128
        results = []
        quarter = self.half // 4
        for columns, first in ((total[:, :cut], 4), (total[:, cut:], 2)):
            if first == 4:
                kept, sent = columns[: 2 * quarter], columns[2 * quarter :]
            else:
                kept = jnp.concatenate([columns[:quarter], columns[2 * quarter : 3 * quarter]])
                sent = jnp.concatenate([columns[quarter : 2 * quarter], columns[3 * quarter :]])
            columns = kept + self.hop(sent.astype(low), first).astype(jnp.float32)
            for bit in (6 - first, 16, 8):
                if bit == 16:
                    columns = after(columns, earlier)
                middle = columns.shape[0] // 2
                got = self.hop(columns[middle:].astype(low), bit)
                columns = columns[:middle] + got.astype(jnp.float32)
            results.append(columns)
        return jnp.concatenate(results, axis=1)

    def total(self, values, earlier):
        if not self.relative:
            return lax.psum(values, ("fsdp", "rep"))
        for bit in (1, 2, 4, 8, 16):
            if bit == 8:
                values = after(values, earlier)
            values = values + self.hop(values, bit)
        return values

    def own(self, values):
        device = lax.axis_index("fsdp") * self.rep + lax.axis_index("rep")
        return lax.dynamic_slice_in_dim(values, device * self.own_rows, self.own_rows, 0)


def scatter_rep(piece_of, size):
    me = lax.axis_index("rep")
    low = jnp.bfloat16
    far_near = swap(piece_of(me ^ 3).astype(low), "rep", size, 1)
    near = swap(piece_of(me ^ 1).astype(low), "rep", size, 1)
    far = (piece_of(me ^ 2) + far_near.astype(jnp.float32)).astype(low)
    far = swap(far, "rep", size, 2)
    return piece_of(me) + near.astype(jnp.float32), far


def add_late(near_sum, far, earlier):
    near_sum, far = lax.optimization_barrier((near_sum, far, earlier))[:2]
    return near_sum + far.astype(jnp.float32)


def shards(
    fsdp,
    rep,
    tokens,
    attn_gain,
    qkv_weight,
    out_weight,
    ffn_gain,
    router_weight,
    expert_in,
    expert_out,
    bias_table,
    seq_lengths,
    bucket_map,
    expert_ids,
    cotangent,
):
    row_count, model_width = tokens.shape
    head_count, buckets = bias_table.shape
    head_size = model_width // head_count
    experts = router_weight.shape[1]
    capacity = 4 * row_count // experts
    highest = lax.Precision.HIGHEST
    own_rows, qkv_width = qkv_weight.shape
    extra = -(-(experts + 2) // LANES) * LANES
    me = lax.axis_index("fsdp")
    ring = Ring(fsdp, rep, own_rows)
    cut = qkv_width // 2

    small = jnp.concatenate(
        [
            router_weight,
            attn_gain[:, None],
            ffn_gain[:, None],
            jnp.zeros((own_rows, extra - experts - 2), jnp.bfloat16),
        ],
        axis=1,
    )
    line_qkv = ring.line(jnp.concatenate([qkv_weight, small], axis=1))
    first, second = ring.gather(line_qkv, cut)
    weight_out = lax.all_gather(out_weight, ("fsdp", "rep"), axis=0, tiled=True)

    position = slot_position(expert_ids, experts)
    slot_ids = expert_ids * capacity + position
    group_ids = ring.group(expert_ids)
    to_me = group_ids == me
    named = jnp.any(to_me, axis=2)
    other_ids = jnp.where(to_me[:, :, 0], group_ids[:, :, 1], group_ids[:, :, 0])
    places = jnp.where(named, jnp.cumsum(named, axis=1, dtype=jnp.int32) - 1, -1)
    slot_others = jnp.sum(
        jnp.where(
            places[:, None, :] == jnp.arange(capacity, dtype=jnp.int32)[None, :, None],
            other_ids[:, None, :],
            0,
        ),
        axis=2,
    )
    slot_others = ring.by_source(slot_others)
    slot_ids_across = slot_ids.T

    feature = jnp.arange(model_width, dtype=jnp.int32)
    picks = [
        (ring.order(which)[:, None] == feature[None, :]).astype(jnp.bfloat16) for which in range(2)
    ]
    pick = jnp.concatenate(picks)
    tokens_rel = times_trans(tokens, pick).astype(jnp.bfloat16)
    onehot = distance_onehot(bucket_map, row_count, buckets)
    base = lax.dot_general(bias_table, onehot, (((1,), (1,)), ((), ())), precision=highest)
    starts = sequence_starts(seq_lengths[0], row_count)

    sent_dy = spread(slot_ids_across, cotangent, experts, capacity)
    slot_dy = trade(after(sent_dy, line_qkv))
    weight_in = lax.all_gather(expert_in, "rep", axis=1, tiled=True)[0]
    weight_back = lax.all_gather(expert_out, "rep", axis=1, tiled=True)[0]

    def natural(halves):
        joined = trans_times(pick, jnp.concatenate(halves))
        return joined.astype(jnp.bfloat16)

    packed, *normed_halves = project(tokens_rel, first, second, experts, qkv_width)
    small = natural([half[:, qkv_width - cut :] for half in second])
    gains = small.T.astype(jnp.float32)
    gain_one, gain_two = gains[experts : experts + 1], gains[experts + 1 : experts + 2]
    attended, levels = attention(base, starts, packed, head_size)
    mixed, normed_two, *sending = mix(
        slot_ids_across, tokens, attended, weight_out, gain_two, experts, capacity
    )
    place = me[None].astype(jnp.int32)
    size = capacity // PARTS
    arrived = [trade(after(sending[0], slot_dy))]
    arrived.append(trade(after(sending[1], arrived[0])))
    payloads, kept = [], None
    for part in range(PARTS):
        payload, kept = expert_rows(
            place,
            part,
            arrived[part],
            slot_dy,
            slot_others[:, part * size : (part + 1) * size].reshape(-1, 1),
            small,
            weight_in,
            weight_back,
            kept,
        )
        payloads.append(payload)
    produced, rows_all, slot_grad, active, d_hidden, unused_tails = kept
    payloads[0] = trade(payloads[0])
    payloads[1] = trade(after(payloads[1], payloads[0]))
    rows_all, slot_grad, active, d_hidden = lax.optimization_barrier(
        (rows_all, slot_grad, active, d_hidden, payloads[0])
    )[:4]
    returned = trade(after(produced, payloads[1]))

    in_rows = expert_in.shape[1]
    out_rows = expert_out.shape[1]
    owned_in = scatter_rep(
        lambda who: trans_times(
            lax.dynamic_slice_in_dim(rows_all, who * in_rows, in_rows, 1), d_hidden
        ),
        rep,
    )
    owned_out = scatter_rep(
        lambda who: trans_times(
            lax.dynamic_slice_in_dim(active, who * out_rows, out_rows, 1), slot_grad
        ),
        rep,
    )

    attended_rel = times_trans(attended, pick).astype(jnp.bfloat16)
    normed_rel = times_trans(normed_two, pick).astype(jnp.bfloat16)
    d_mixed, d_attended, gates, *out_pieces = collect(
        slot_ids,
        expert_ids,
        normed_two,
        mixed,
        cotangent,
        small,
        gain_two,
        weight_out,
        pick,
        attended_rel,
        normed_rel,
        payloads,
    )
    d_packed, d_base, *pieces = attention_pull(
        base, starts, packed, d_attended, levels, normed_halves, out_pieces, head_size
    )
    owned = ring.scatter(*pieces, returned)
    weight_qkv = jnp.concatenate(
        [natural(first), natural([half[:, : qkv_width - cut] for half in second])], axis=1
    )
    d_normed_one = times_trans(d_packed, weight_qkv)
    inputs = tokens.astype(jnp.float32)
    unused_one, norm_pull_one = jax.vjp(rms_norm, inputs, gain_one)
    d_inputs_norm, d_gain_one = norm_pull_one(d_normed_one)
    token_grad = d_mixed + d_inputs_norm
    bias_local = jnp.dot(d_base, onehot, precision=highest)
    late = jnp.concatenate([d_gain_one.reshape(-1), bias_local.reshape(-1)])
    late = ring.total(late, returned)
    output = finish(slot_ids, gates, mixed, returned)
    return (
        output,
        token_grad,
        ring.own(late[:model_width]),
        owned[:, :qkv_width],
        owned[:, qkv_width : qkv_width + model_width],
        owned[:, -1],
        owned[:, qkv_width + model_width : qkv_width + model_width + experts],
        add_late(*owned_in, d_packed)[None],
        add_late(*owned_out, d_packed)[None],
        late[model_width:].reshape(bias_table.shape),
    )


def solution(mesh):
    return jax.shard_map(
        functools.partial(shards, mesh.shape["fsdp"], mesh.shape["rep"]),
        mesh=mesh,
        in_specs=(
            P(("fsdp", "rep"), None),
            P(("fsdp", "rep")),
            P(("fsdp", "rep"), None),
            P(("fsdp", "rep"), None),
            P(("fsdp", "rep")),
            P(("fsdp", "rep"), None),
            P("fsdp", "rep", None),
            P("fsdp", "rep", None),
            P(),
            P(("fsdp", "rep"), None),
            P(),
            P(("fsdp", "rep"), None),
            P(("fsdp", "rep"), None),
        ),
        out_specs=(
            P(("fsdp", "rep"), None),
            P(("fsdp", "rep"), None),
            P(("fsdp", "rep")),
            P(("fsdp", "rep"), None),
            P(("fsdp", "rep"), None),
            P(("fsdp", "rep")),
            P(("fsdp", "rep"), None),
            P("fsdp", "rep", None),
            P("fsdp", "rep", None),
            P(),
        ),
        check_vma=False,
    )
```

```python
import functools

import jax
import jax.numpy as jnp
from jax import lax
from jax.experimental import pallas as pl
from jax.experimental.pallas import tpu as pltpu
from jax.sharding import PartitionSpec as P

EPSILON = 1e-06
MASKED = -1e30
GELU_COEF = 0.7978845608028654
TILE = 128
LANES = 128
PARTS = 2
TAIL = 16
VMEM_BYTES = 56 * 1024 * 1024


def rms_norm(values, gain_vector):
    return (
        values
        * lax.rsqrt(jnp.mean(values * values, axis=-1, keepdims=True) + EPSILON)
        * gain_vector
    )


def times(left_side, right_side):
    return lax.dot_general(
        left_side, right_side, (((1,), (0,)), ((), ())), preferred_element_type=jnp.float32
    )


def times_trans(left_side, right_side):
    return lax.dot_general(
        left_side, right_side, (((1,), (1,)), ((), ())), preferred_element_type=jnp.float32
    )


def trans_times(left_side, right_side):
    return lax.dot_general(
        left_side, right_side, (((0,), (0,)), ((), ())), preferred_element_type=jnp.float32
    )


def sequence_starts(lengths, row_count):
    seq_ends = jnp.cumsum(lengths, dtype=jnp.int32)
    places = jnp.arange(row_count, dtype=jnp.int32)
    passed = places[:, None] >= seq_ends[None, :]
    return jnp.max(jnp.where(passed, seq_ends[None, :], 0), axis=1, keepdims=True)


def distance_onehot(bucket_map, row_count, buckets):
    longest = bucket_map.shape[0]
    distance = row_count - TILE - jnp.arange(row_count, dtype=jnp.int32)
    place = jnp.arange(longest, dtype=jnp.int32)
    at_distance = jnp.sum(
        jnp.where(distance[:, None] == place[None, :], bucket_map[None, :] + 1, 0), axis=1
    )
    return (at_distance[:, None] == 1 + jnp.arange(buckets, dtype=jnp.int32)[None, :]).astype(
        jnp.float32
    )


def head_lanes(block, which, head_size):
    lane = lax.broadcasted_iota(jnp.int32, block.shape, 1)
    inside = (lane >= which * head_size) & (lane < (which + 1) * head_size)
    return jnp.where(inside, block, jnp.zeros_like(block))


def bias_strip(base_ref, head, row_count):
    row = base_ref[pl.ds(head, 1), :]
    spread = jnp.broadcast_to(row, (TILE, row_count))
    return pltpu.roll(spread, 0, 1, stride=1, stride_axis=0)


def tile_score(query_tile, keys, strip, starts, tile, scale):
    row_count = strip.shape[1]
    width = TILE * (tile + 1)
    score = times_trans(query_tile, keys[:width]) * scale + strip[:, row_count - width :]
    place = lax.broadcasted_iota(jnp.int32, score.shape, 1)
    row = lax.broadcasted_iota(jnp.int32, score.shape, 0) + TILE * tile
    return jnp.where((place <= row) & (place >= starts), score, MASKED)


def lane_block(first):
    return pl.ds(pl.multiple_of(first, LANES), LANES)


def attention_kernel(head_size, base_ref, starts_ref, packed_ref, attended_ref, level_ref):
    row_count, width = attended_ref.shape
    per_block = LANES // head_size
    scale = head_size ** (-0.5)

    @pl.loop(0, width // LANES)
    def _(block):
        queries = packed_ref[:, lane_block(block * LANES)]
        keys = packed_ref[:, lane_block(width + block * LANES)]
        values = packed_ref[:, lane_block(2 * width + block * LANES)]
        strips = [bias_strip(base_ref, block * per_block + own, row_count) for own in range(per_block)]
        for tile in range(row_count // TILE):
            rows = slice(tile * TILE, (tile + 1) * TILE)
            starts = starts_ref[rows, :]
            total = jnp.zeros((TILE, LANES), jnp.float32)
            for own in range(per_block):
                score = tile_score(
                    head_lanes(queries[rows], own, head_size), keys, strips[own], starts, tile, scale
                )
                peak = jnp.max(score, axis=1, keepdims=True)
                exponent = jnp.exp(score - peak)
                whole = jnp.sum(exponent, axis=1, keepdims=True)
                level_ref[block, rows, own : own + 1] = peak + jnp.log(whole)
                probs = (exponent * (1.0 / whole)).astype(jnp.bfloat16)
                total += times(probs, head_lanes(values[: probs.shape[1]], own, head_size))
            attended_ref[rows, lane_block(block * LANES)] = total.astype(jnp.bfloat16)


def attention(base, starts, packed, head_size):
    row_count = packed.shape[0]
    width = packed.shape[1] // 3
    return pl.pallas_call(
        functools.partial(attention_kernel, head_size),
        out_shape=(
            jax.ShapeDtypeStruct((row_count, width), jnp.bfloat16),
            jax.ShapeDtypeStruct((width // LANES, row_count, LANES // head_size), jnp.float32),
        ),
        compiler_params=pltpu.CompilerParams(vmem_limit_bytes=VMEM_BYTES),
        cost_estimate=pl.CostEstimate(flops=1000, bytes_accessed=1000, transcendentals=0),
        name="attention",
    )(base, starts, packed)


def attention_pull_kernel(
    head_size,
    base_ref,
    starts_ref,
    packed_ref,
    grad_ref,
    level_ref,
    kept_rows_ref,
    sent_rows_ref,
    out_keep_ref,
    out_send_ref,
    d_packed_ref,
    d_base_ref,
    keep_ref,
    send_ref,
    d_keys_ref,
    d_values_ref,
    d_strip_ref,
):
    row_count, width = grad_ref.shape
    per_block = LANES // head_size
    scale = head_size ** (-0.5)

    @pl.loop(0, width // LANES)
    def _(block):
        queries = packed_ref[:, lane_block(block * LANES)]
        keys = packed_ref[:, lane_block(width + block * LANES)]
        values = packed_ref[:, lane_block(2 * width + block * LANES)]
        grads = grad_ref[:, lane_block(block * LANES)]
        strips = [bias_strip(base_ref, block * per_block + own, row_count) for own in range(per_block)]
        d_keys_ref[...] = jnp.zeros_like(d_keys_ref)
        d_values_ref[...] = jnp.zeros_like(d_values_ref)
        d_strip_ref[...] = jnp.zeros_like(d_strip_ref)
        for tile in range(row_count // TILE):
            rows = slice(tile * TILE, (tile + 1) * TILE)
            reach = TILE * (tile + 1)
            starts = starts_ref[rows, :]
            d_queries = jnp.zeros((TILE, LANES), jnp.float32)
            for own in range(per_block):
                own_queries = head_lanes(queries[rows], own, head_size)
                own_grads = head_lanes(grads[rows], own, head_size)
                score = tile_score(own_queries, keys, strips[own], starts, tile, scale)
                probs = jnp.exp(score - level_ref[block, rows, own : own + 1])
                d_probs = times_trans(own_grads, values[:reach])
                row_delta = jnp.sum(probs * d_probs, axis=1, keepdims=True)
                d_score = (probs * (d_probs - row_delta)).astype(jnp.bfloat16)
                d_strip_ref[own, :, row_count - reach :] += d_score.astype(jnp.float32)
                d_queries += times(d_score, head_lanes(keys[:reach], own, head_size))
                d_keys_ref[:reach, :] += trans_times(d_score, own_queries)
                d_values_ref[:reach, :] += trans_times(probs.astype(jnp.bfloat16), own_grads)
            d_packed_ref[rows, lane_block(block * LANES)] = (d_queries * scale).astype(jnp.bfloat16)
        d_packed_ref[:, lane_block(width + block * LANES)] = (d_keys_ref[...] * scale).astype(
            jnp.bfloat16
        )
        d_packed_ref[:, lane_block(2 * width + block * LANES)] = d_values_ref[...].astype(
            jnp.bfloat16
        )
        for own in range(per_block):
            folded = d_strip_ref[own]
            half = TILE // 2
            while half >= 8:
                folded = folded[:half] + pltpu.roll(folded[half:], row_count - half, 1)
                half //= 2
            row = lax.broadcasted_iota(jnp.int32, folded.shape, 0)
            for bit in (4, 2, 1):
                folded = jnp.where(
                    (row & bit) != 0, pltpu.roll(folded, row_count - bit, 1), folded
                )
            d_base_ref[pl.ds(block * per_block + own, 1), :] = jnp.sum(
                folded, axis=0, keepdims=True
            )

    keep_ref[:, 3 * width :] = out_keep_ref[...]
    send_ref[:, 3 * width :] = out_send_ref[...]
    for start in range(0, 3 * width, width):
        columns = slice(start, start + width)
        send_ref[:, columns] = trans_times(sent_rows_ref[...], d_packed_ref[:, columns]).astype(
            jnp.bfloat16
        )
        keep_ref[:, columns] = trans_times(kept_rows_ref[...], d_packed_ref[:, columns])


def attention_pull(base, starts, packed, grads, levels, rows, out_pieces, head_size):
    row_count = grads.shape[0]
    half = rows[0].shape[1]
    columns = packed.shape[1] + out_pieces[0].shape[1]
    shape = jax.ShapeDtypeStruct
    return pl.pallas_call(
        functools.partial(attention_pull_kernel, head_size),
        out_shape=(
            shape(packed.shape, jnp.bfloat16),
            shape(base.shape, jnp.float32),
            shape((half, columns), jnp.float32),
            shape((half, columns), jnp.bfloat16),
        ),
        scratch_shapes=[
            pltpu.VMEM((row_count, LANES), jnp.float32),
            pltpu.VMEM((row_count, LANES), jnp.float32),
            pltpu.VMEM((LANES // head_size, TILE, row_count), jnp.float32),
        ],
        compiler_params=pltpu.CompilerParams(vmem_limit_bytes=VMEM_BYTES),
        cost_estimate=pl.CostEstimate(flops=1000, bytes_accessed=1000, transcendentals=0),
        name="attention_pull",
    )(base, starts, packed, grads, levels, *rows, *out_pieces)


def gelu_parts(values):
    inner = GELU_COEF * (values + 0.044715 * values * values * values)
    bend = jnp.tanh(inner)
    slope = 0.5 * (1.0 + bend) + 0.5 * values * (1.0 - bend * bend) * (
        GELU_COEF * (1.0 + 3.0 * 0.044715 * values * values)
    )
    return 0.5 * values * (1.0 + bend), slope


def vmem():
    return pl.BlockSpec(memory_space=pltpu.VMEM)


def two_gates(logits, first_ids, second_ids):
    column = lax.broadcasted_iota(jnp.int32, logits.shape, 1)
    first = jnp.sum(jnp.where(column == first_ids, logits, 0.0), axis=1, keepdims=True)
    second = jnp.sum(jnp.where(column == second_ids, logits, 0.0), axis=1, keepdims=True)
    peak = jnp.maximum(first, second)
    first, second = jnp.exp(first - peak), jnp.exp(second - peak)
    return first / (first + second), second / (first + second)


def project_kernel(column, tokens_ref, *refs):
    first_refs, second_refs = refs[0:2], refs[2:4]
    packed_ref, normed_refs = refs[4], refs[5:7]
    row_count, half = normed_refs[0].shape
    cut = first_refs[0].shape[1]
    rest = packed_ref.shape[1] - cut
    inputs = tokens_ref[...].astype(jnp.float32)
    inverse = lax.rsqrt(jnp.mean(inputs * inputs, axis=1, keepdims=True) + EPSILON)
    for which in range(2):
        small = second_refs[which][:, rest:].astype(jnp.float32)
        gain = jnp.transpose(small)[column : column + 1, :]
        normed = (inputs[:, which * half : (which + 1) * half] * inverse * gain).astype(
            jnp.bfloat16
        )
        normed_refs[which][...] = normed
    both = jnp.concatenate([normed_refs[0][...], normed_refs[1][...]], axis=1)
    for refs_of, start, width in ((first_refs, 0, cut), (second_refs, cut, rest)):
        weights = jnp.concatenate([refs_of[0][:, :width], refs_of[1][:, :width]], axis=0)
        packed_ref[:, start : start + width] = times(both, weights).astype(jnp.bfloat16)


def project(tokens_rel, first, second, column, qkv_width):
    row_count, width = tokens_rel.shape
    half = jax.ShapeDtypeStruct((row_count, width // 2), jnp.bfloat16)
    return pl.pallas_call(
        functools.partial(project_kernel, column),
        out_shape=(jax.ShapeDtypeStruct((row_count, qkv_width), jnp.bfloat16), half, half),
        compiler_params=pltpu.CompilerParams(vmem_limit_bytes=VMEM_BYTES),
        cost_estimate=pl.CostEstimate(flops=1000, bytes_accessed=1000, transcendentals=0),
        name="project",
    )(tokens_rel, *first, *second)


def slot_rows_of(ids_ref, rows, first_place, count):
    place = first_place + lax.broadcasted_iota(jnp.int32, (count, rows.shape[0]), 0)
    inside = (place == ids_ref[0:1, :]) | (place == ids_ref[1:2, :])
    return times(jnp.where(inside, 1.0, 0.0).astype(jnp.bfloat16), rows).astype(jnp.bfloat16)


def fill_blocks(ids_ref, rows, block_refs):
    experts, count, _ = block_refs[0].shape
    for part, block_ref in enumerate(block_refs):
        for expert in range(experts):
            place = (expert * len(block_refs) + part) * count
            block_ref[expert] = slot_rows_of(ids_ref, rows, place, count)


def spread_kernel(ids_ref, rows_ref, block_ref):
    fill_blocks(ids_ref, rows_ref[...], [block_ref])


def spread(slot_ids, rows, experts, capacity):
    row_count, width = rows.shape
    return pl.pallas_call(
        spread_kernel,
        out_shape=jax.ShapeDtypeStruct((experts, capacity, width), jnp.bfloat16),
        compiler_params=pltpu.CompilerParams(vmem_limit_bytes=VMEM_BYTES),
        cost_estimate=pl.CostEstimate(flops=1000, bytes_accessed=1000, transcendentals=0),
        name="spread",
    )(slot_ids, rows)


def mix_kernel(
    ids_ref, tokens_ref, attended_ref, out_ref, gain_ref, mixed_ref, normed_ref, *block_refs
):
    mixed = tokens_ref[...].astype(jnp.float32) + times(attended_ref[...], out_ref[...])
    mixed_ref[...] = mixed
    inverse = lax.rsqrt(jnp.mean(mixed * mixed, axis=1, keepdims=True) + EPSILON)
    normed_ref[...] = (mixed * inverse * gain_ref[...]).astype(jnp.bfloat16)
    fill_blocks(ids_ref, normed_ref[...], block_refs)


def mix(slot_ids, tokens, attended, weight_out, gain, experts, capacity):
    row_count, width = tokens.shape
    block = jax.ShapeDtypeStruct((experts, capacity // PARTS, width), jnp.bfloat16)
    return pl.pallas_call(
        mix_kernel,
        out_shape=(
            jax.ShapeDtypeStruct((row_count, width), jnp.float32),
            jax.ShapeDtypeStruct((row_count, width), jnp.bfloat16),
        )
        + (block,) * PARTS,
        compiler_params=pltpu.CompilerParams(vmem_limit_bytes=VMEM_BYTES),
        cost_estimate=pl.CostEstimate(flops=1000, bytes_accessed=1000, transcendentals=0),
        name="mix",
    )(slot_ids, tokens, attended, weight_out, gain)


def expert_kernel(
    part,
    place_ref,
    rows_ref,
    grads_ref,
    other_ref,
    router_ref,
    in_ref,
    out_ref,
    *refs,
):
    payload_ref, produced_ref, rows_all, slot_grad_all, active_ref, d_hidden_ref = refs[-11:-5]
    tails_ref = refs[-5] if part == 0 else refs[0]
    rows, slot_grad, produced_sum, row_sum = refs[-4:]
    sources, capacity, width = rows_ref.shape
    count = sources * capacity
    step = pl.program_id(0)

    @pl.when(step == 0)
    def _():
        rows[...] = rows_ref[...].reshape(count, width)
        logits = times(rows[...], router_ref[...])
        own_ids = jnp.full((count, 1), place_ref[0], jnp.int32)
        gate, unused_gate = two_gates(logits, own_ids, other_ref[...])
        grads = grads_ref[...].reshape(count, width).astype(jnp.float32)
        slot_grad[...] = (gate * grads).astype(jnp.bfloat16)
        rows_all[...] = rows[...]
        slot_grad_all[...] = slot_grad[...]
        produced_sum[...] = jnp.zeros_like(produced_sum)
        row_sum[...] = jnp.zeros_like(row_sum)

    hidden = times(rows[...], in_ref[...])
    active, slope = gelu_parts(hidden)
    active = active.astype(jnp.bfloat16)
    active_ref[...] = active
    d_active = times_trans(slot_grad[...], out_ref[...])
    d_hidden = (slope * d_active).astype(jnp.bfloat16)
    d_hidden_ref[...] = d_hidden
    produced_sum[...] += times(active, out_ref[...])
    row_sum[...] += times_trans(d_hidden, in_ref[...])

    @pl.when(step == pl.num_programs(0) - 1)
    def _():
        for source in range(sources):
            own = slice(source * capacity, (source + 1) * capacity)
            result = produced_sum[own, :].astype(jnp.bfloat16)
            produced_ref[source] = result
            payload_ref[source, :capacity, :] = row_sum[own, :].astype(jnp.bfloat16)
            d_gate = jnp.sum(
                result.astype(jnp.float32) * grads_ref[source].astype(jnp.float32),
                axis=1,
                keepdims=True,
            )
            across = jnp.transpose(jnp.broadcast_to(d_gate, (capacity, LANES)))[:TAIL, :]
            high = across.astype(jnp.bfloat16).astype(jnp.float32)
            row = lax.broadcasted_iota(jnp.int32, across.shape, 0) - 2 * part
            tail = jnp.where(row == 0, high, jnp.where(row == 1, across - high, 0.0))
            if part == 0:
                tails_ref[source, :, :] = tail
            else:
                tail = (tails_ref[source, :, :] + tail).astype(jnp.bfloat16)
                payload_ref[source, capacity:, :] = jnp.zeros((TAIL, width), jnp.bfloat16)
                payload_ref[source, capacity:, :capacity] = tail


def expert_rows(place, part, rows, grads, other, router, weight_in, weight_out, earlier):
    sources, capacity, width = rows.shape
    hidden_width = weight_in.shape[1]
    chunk = hidden_width // 4
    count = sources * capacity

    def whole(shape):
        return pl.BlockSpec(shape, lambda i, place: (0,) * len(shape))

    def part_of(*shape):
        return pl.BlockSpec(shape, lambda i, place: (0, part, 0))

    def part_block(columns):
        return pl.BlockSpec((count, columns), lambda i, place: (part, 0))

    def part_chunk():
        return pl.BlockSpec((count, chunk), lambda i, place: (part, i))

    def full(*shape):
        return jax.ShapeDtypeStruct(shape, jnp.bfloat16)

    total = PARTS * count
    operands = (rows, grads, other, router, weight_in, weight_out)
    in_specs = [
        whole(rows.shape),
        part_of(sources, capacity, width),
        whole(other.shape),
        whole(router.shape),
        pl.BlockSpec((width, chunk), lambda i, place: (0, i)),
        pl.BlockSpec((chunk, width), lambda i, place: (i, 0)),
    ]
    aliases = {}
    if earlier is not None:
        earlier, tails = earlier[:-1], earlier[-1]
        operands = operands + (tails,)
        in_specs = in_specs + [whole(tails.shape)]
        aliases = {1 + len(operands) + which: 1 + which for which in range(5)}
        operands = operands + tuple(earlier)
        in_specs = in_specs + [pl.BlockSpec(memory_space=pl.ANY)] * 5
    results = pl.pallas_call(
        functools.partial(expert_kernel, part),
        grid_spec=pltpu.PrefetchScalarGridSpec(
            num_scalar_prefetch=1,
            grid=(4,),
            in_specs=in_specs,
            out_specs=[
                whole((sources, capacity + part * TAIL, width)),
                part_of(sources, capacity, width),
                part_block(width),
                part_block(width),
                part_chunk(),
                part_chunk(),
                whole((sources, TAIL, capacity)),
            ],
            scratch_shapes=[
                pltpu.VMEM((count, width), jnp.bfloat16),
                pltpu.VMEM((count, width), jnp.bfloat16),
                pltpu.VMEM((count, width), jnp.float32),
                pltpu.VMEM((count, width), jnp.float32),
            ],
        ),
        out_shape=[
            full(sources, capacity + part * TAIL, width),
            full(sources, PARTS * capacity, width),
            full(total, width),
            full(total, width),
            full(total, hidden_width),
            full(total, hidden_width),
            jax.ShapeDtypeStruct((sources, TAIL, capacity), jnp.float32),
        ],
        input_output_aliases=aliases,
        compiler_params=pltpu.CompilerParams(vmem_limit_bytes=VMEM_BYTES),
        cost_estimate=pl.CostEstimate(
            flops=8 * count * width * hidden_width,
            bytes_accessed=4 * count * (hidden_width + 4 * width) + 4 * width * hidden_width,
            transcendentals=count * hidden_width,
        ),
        name="expert_rows",
    )(place, *operands)
    return results[0], results[1:]


def collect_kernel(
    slots_ref,
    experts_ref,
    places_ref,
    normed_ref,
    mixed_ref,
    cotangent_ref,
    router_ref,
    gain_ref,
    out_ref,
    pick_ref,
    attended_ref,
    normed_rel_ref,
    *refs,
):
    payload_refs = refs[:-5]
    d_mixed_ref, d_attended_ref, gates_ref, keep_ref, send_ref = refs[-5:]
    row_count, width = mixed_ref.shape
    experts, capacity, _ = payload_refs[0].shape
    first_slots, second_slots = slots_ref[:, 0:1], slots_ref[:, 1:2]
    first_grad = jnp.zeros((row_count, 1), jnp.float32)
    second_grad = jnp.zeros((row_count, 1), jnp.float32)
    d_normed = jnp.zeros((row_count, width), jnp.float32)
    for part, payload_ref in enumerate(payload_refs):
        places = places_ref[part : part + 1, :]
        select = jnp.where((places == first_slots) | (places == second_slots), 1.0, 0.0)
        d_normed += times(select.astype(jnp.bfloat16), payload_ref[:, :capacity, :].reshape(-1, width))
        for expert in range(experts):
            first_place = (expert * len(payload_refs) + part) * capacity
            place = first_place + lax.broadcasted_iota(jnp.int32, (row_count, capacity), 1)
            tail = payload_refs[-1][expert, capacity:, :capacity].astype(jnp.float32)
            d_gate = tail[2 * part : 2 * part + 1, :] + tail[2 * part + 1 : 2 * part + 2, :]
            first_grad += jnp.sum(
                jnp.where(place == first_slots, d_gate, 0.0), axis=1, keepdims=True
            )
            second_grad += jnp.sum(
                jnp.where(place == second_slots, d_gate, 0.0), axis=1, keepdims=True
            )
    logits = times(normed_ref[...], router_ref[...])
    first_ids, second_ids = experts_ref[:, 0:1], experts_ref[:, 1:2]
    first_gate, second_gate = two_gates(logits, first_ids, second_ids)
    mean = first_gate * first_grad + second_gate * second_grad
    column = lax.broadcasted_iota(jnp.int32, logits.shape, 1)
    d_logits = jnp.where(
        column == first_ids,
        first_gate * (first_grad - mean),
        jnp.where(column == second_ids, second_gate * (second_grad - mean), 0.0),
    ).astype(jnp.bfloat16)
    gates_ref[:, 0:1] = first_gate
    gates_ref[:, 1:2] = second_gate
    d_normed = d_normed + times_trans(d_logits, router_ref[...])
    mixed = mixed_ref[...]
    inverse = lax.rsqrt(jnp.mean(mixed * mixed, axis=1, keepdims=True) + EPSILON)
    d_gain = jnp.sum(d_normed * mixed * inverse, axis=0, keepdims=True)
    scaled = d_normed * gain_ref[...]
    pulled = jnp.mean(scaled * mixed, axis=1, keepdims=True) * inverse * inverse
    d_mixed = cotangent_ref[...].astype(jnp.float32) + inverse * (scaled - mixed * pulled)
    d_mixed_ref[...] = d_mixed
    d_branch = d_mixed.astype(jnp.bfloat16)
    d_attended_ref[...] = times_trans(d_branch, out_ref[...]).astype(jnp.bfloat16)
    small = trans_times(normed_rel_ref[...], d_logits)
    column = lax.broadcasted_iota(jnp.int32, small.shape, 1)
    gain_column = jnp.sum(
        pick_ref[...].astype(jnp.float32) * d_gain, axis=1, keepdims=True
    )
    small = jnp.where(column == small.shape[1] - 1, gain_column, small)
    half = width // 2
    keep_ref[:, width:] = small[:half]
    send_ref[:, width:] = small[half:].astype(jnp.bfloat16)
    keep_ref[:, :width] = trans_times(attended_ref[:, :half], d_branch)
    send_ref[:, :width] = trans_times(attended_ref[:, half:], d_branch).astype(jnp.bfloat16)


def collect(
    slots,
    experts,
    normed,
    mixed,
    cotangent,
    router,
    gain,
    weight_out,
    pick,
    attended_rel,
    normed_rel,
    payloads,
):
    row_count, width = mixed.shape
    sources, size, _ = payloads[0].shape
    places = (
        (jnp.arange(sources, dtype=jnp.int32)[None, :, None] * len(payloads)
        + jnp.arange(len(payloads), dtype=jnp.int32)[:, None, None])
        * size
        + jnp.arange(size, dtype=jnp.int32)[None, None, :]
    ).reshape(len(payloads), sources * size)
    columns = width + router.shape[1]
    return pl.pallas_call(
        collect_kernel,
        out_shape=(
            jax.ShapeDtypeStruct((row_count, width), jnp.float32),
            jax.ShapeDtypeStruct((row_count, width), jnp.bfloat16),
            jax.ShapeDtypeStruct((row_count, 2), jnp.float32),
            jax.ShapeDtypeStruct((width // 2, columns), jnp.float32),
            jax.ShapeDtypeStruct((width // 2, columns), jnp.bfloat16),
        ),
        compiler_params=pltpu.CompilerParams(vmem_limit_bytes=VMEM_BYTES),
        cost_estimate=pl.CostEstimate(flops=1000, bytes_accessed=1000, transcendentals=0),
        name="collect",
    )(
        slots,
        experts,
        places,
        normed,
        mixed,
        cotangent,
        router,
        gain,
        weight_out,
        pick,
        attended_rel,
        normed_rel,
        *payloads,
    )


def finish_kernel(slots_ref, gates_ref, mixed_ref, produced_ref, output_ref):
    row_count, width = mixed_ref.shape
    experts, capacity, _ = produced_ref.shape
    produced = produced_ref[...].reshape(experts * capacity, width)
    place = lax.broadcasted_iota(jnp.int32, (row_count, experts * capacity), 1)
    total = mixed_ref[...]
    for which in range(2):
        select = jnp.where(place == slots_ref[:, which : which + 1], 1.0, 0.0)
        found = times(select.astype(jnp.bfloat16), produced)
        total = total + gates_ref[:, which : which + 1] * found
    output_ref[...] = total.astype(jnp.bfloat16)


def finish(slots, gates, mixed, produced):
    row_count, width = mixed.shape
    return pl.pallas_call(
        finish_kernel,
        out_shape=jax.ShapeDtypeStruct((row_count, width), jnp.bfloat16),
        compiler_params=pltpu.CompilerParams(vmem_limit_bytes=VMEM_BYTES),
        cost_estimate=pl.CostEstimate(flops=1000, bytes_accessed=1000, transcendentals=0),
        name="finish",
    )(slots, gates, mixed, produced)


def slot_position(device_ids, experts):
    flat_ids = device_ids.reshape(-1)
    chosen = (flat_ids[:, None] == jnp.arange(experts, dtype=jnp.int32)[None, :]).astype(jnp.int32)
    before = jnp.cumsum(chosen, axis=0, dtype=jnp.int32) - chosen
    position = jnp.sum(before * chosen, axis=1, dtype=jnp.int32)
    return position.reshape(device_ids.shape)


def swap(rows, axis, size, step):
    return lax.ppermute(rows, axis, [(index, index ^ step) for index in range(size)])


def after(values, *earlier):
    return lax.optimization_barrier((values,) + earlier)[0]


def trade(blocks):
    return lax.all_to_all(blocks, "fsdp", split_axis=0, concat_axis=0, tiled=True)


class Ring:
    def __init__(self, fsdp, rep, own_rows):
        self.fsdp, self.rep, self.own_rows = fsdp, rep, own_rows
        self.relative = fsdp == 8 and rep == 4
        self.half = own_rows * fsdp * rep // 2

    def order(self, which):
        row = jnp.arange(self.half, dtype=jnp.int32)
        if not self.relative:
            return row + which * self.half
        group = row // self.own_rows
        mask = which + 8 * (group & 1) + 16 * ((group >> 1) & 1) + 2 * ((group >> 2) & 1)
        mask = mask + 4 * ((group >> 3) & 1)
        device = lax.axis_index("fsdp") * self.rep + lax.axis_index("rep")
        return (device ^ mask) * self.own_rows + row % self.own_rows

    def hop(self, rows, bit):
        return swap(rows, "rep", 4, bit) if bit < 4 else swap(rows, "fsdp", 8, bit // 4)

    def line(self, shard):
        if not self.relative:
            return shard
        return jnp.concatenate([shard] + [self.hop(shard, bit) for bit in (8, 16, 24)])

    def gather(self, line, cut):
        if not self.relative:
            whole = lax.all_gather(line, ("fsdp", "rep"), axis=0, tiled=True)
            halves = (whole[: self.half], whole[self.half :])
            return tuple(h[:, :cut] for h in halves), tuple(h[:, cut:] for h in halves)
        parts = []
        for columns, early, late in ((line[:, :cut], 2, 4), (line[:, cut:], 4, 2)):
            one = self.hop(columns, early)
            two = self.hop(columns, late)
            both = self.hop(one, late)
            by_y, by_x = (one, two) if early == 2 else (two, one)
            parts.append(jnp.concatenate([columns, by_y, by_x, both]))
        return tuple((part, self.hop(part, 1)) for part in parts)

    def group(self, rows):
        if not self.relative:
            return lax.all_gather(rows, "fsdp", axis=0)
        rows = rows[None]
        for bit in (4, 8, 16):
            rows = jnp.concatenate([rows, self.hop(rows, bit)])
        return rows

    def by_source(self, rows):
        if not self.relative:
            return rows
        order = lax.axis_index("fsdp") ^ jnp.arange(self.fsdp, dtype=jnp.int32)
        return jnp.take(rows, order, axis=0)

    def scatter(self, keep, send, earlier, riders):
        if not self.relative:
            whole = jnp.concatenate([keep, send.astype(jnp.float32)])
            whole = lax.psum_scatter(whole, ("fsdp", "rep"), scatter_dimension=0, tiled=True)
            return whole, riders, keep
        total = keep + self.hop(send, 1).astype(jnp.float32)
        total, riders = lax.optimization_barrier((total, riders))
        low = jnp.bfloat16
        cut = -(-total.shape[1] // 256) * 128
        results = []
        quarter = self.half // 4
        for columns, first in ((total[:, :cut], 4), (total[:, cut:], 2)):
            if first == 4:
                kept, sent = columns[: 2 * quarter], columns[2 * quarter :]
            else:
                kept = jnp.concatenate([columns[:quarter], columns[2 * quarter : 3 * quarter]])
                sent = jnp.concatenate([columns[quarter : 2 * quarter], columns[3 * quarter :]])
            columns = kept + self.hop(sent.astype(low), first).astype(jnp.float32)
            mark = columns
            for bit in (6 - first, 16, 8):
                if bit == 16:
                    columns = after(columns, earlier)
                middle = columns.shape[0] // 2
                got = self.hop(columns[middle:].astype(low), bit)
                columns = columns[:middle] + got.astype(jnp.float32)
            results.append(columns)
        return jnp.concatenate(results, axis=1), riders, mark

    def total(self, values, earlier):
        if not self.relative:
            return lax.psum(values, ("fsdp", "rep"))
        for bit in (1, 2, 4, 8, 16):
            if bit == 8:
                values = after(values, earlier)
            values = values + self.hop(values, bit)
        return values

    def own(self, values):
        device = lax.axis_index("fsdp") * self.rep + lax.axis_index("rep")
        return lax.dynamic_slice_in_dim(values, device * self.own_rows, self.own_rows, 0)


def scatter_rep(piece_of, size):
    me = lax.axis_index("rep")
    low = jnp.bfloat16
    far_near = swap(piece_of(me ^ 3).astype(low), "rep", size, 1)
    near = swap(piece_of(me ^ 1).astype(low), "rep", size, 1)
    far = (piece_of(me ^ 2) + far_near.astype(jnp.float32)).astype(low)
    far = swap(far, "rep", size, 2)
    return piece_of(me) + near.astype(jnp.float32), far


def add_late(near_sum, far, earlier):
    near_sum, far = lax.optimization_barrier((near_sum, far, earlier))[:2]
    return near_sum + far.astype(jnp.float32)


def shards(
    fsdp,
    rep,
    tokens,
    attn_gain,
    qkv_weight,
    out_weight,
    ffn_gain,
    router_weight,
    expert_in,
    expert_out,
    bias_table,
    seq_lengths,
    bucket_map,
    expert_ids,
    cotangent,
):
    row_count, model_width = tokens.shape
    head_count, buckets = bias_table.shape
    head_size = model_width // head_count
    experts = router_weight.shape[1]
    capacity = 4 * row_count // experts
    highest = lax.Precision.HIGHEST
    own_rows, qkv_width = qkv_weight.shape
    extra = -(-(experts + 2) // LANES) * LANES
    me = lax.axis_index("fsdp")
    ring = Ring(fsdp, rep, own_rows)
    cut = qkv_width // 2

    small = jnp.concatenate(
        [
            router_weight,
            attn_gain[:, None],
            ffn_gain[:, None],
            jnp.zeros((own_rows, extra - experts - 2), jnp.bfloat16),
        ],
        axis=1,
    )
    line_qkv = ring.line(jnp.concatenate([qkv_weight, small], axis=1))
    first, second = ring.gather(line_qkv, cut)
    weight_out = lax.all_gather(out_weight, ("fsdp", "rep"), axis=0, tiled=True)

    position = slot_position(expert_ids, experts)
    slot_ids = expert_ids * capacity + position
    group_ids = ring.group(expert_ids)
    to_me = group_ids == me
    named = jnp.any(to_me, axis=2)
    other_ids = jnp.where(to_me[:, :, 0], group_ids[:, :, 1], group_ids[:, :, 0])
    places = jnp.where(named, jnp.cumsum(named, axis=1, dtype=jnp.int32) - 1, -1)
    slot_others = jnp.sum(
        jnp.where(
            places[:, None, :] == jnp.arange(capacity, dtype=jnp.int32)[None, :, None],
            other_ids[:, None, :],
            0,
        ),
        axis=2,
    )
    slot_others = ring.by_source(slot_others)
    slot_ids_across = slot_ids.T

    feature = jnp.arange(model_width, dtype=jnp.int32)
    picks = [
        (ring.order(which)[:, None] == feature[None, :]).astype(jnp.bfloat16) for which in range(2)
    ]
    pick = jnp.concatenate(picks)
    tokens_rel = times_trans(tokens, pick).astype(jnp.bfloat16)
    onehot = distance_onehot(bucket_map, row_count, buckets)
    base = lax.dot_general(bias_table, onehot, (((1,), (1,)), ((), ())), precision=highest)
    starts = sequence_starts(seq_lengths[0], row_count)

    sent_dy = spread(slot_ids_across, cotangent, experts, capacity)
    slot_dy = trade(after(sent_dy, line_qkv))
    weight_in = lax.all_gather(expert_in, "rep", axis=1, tiled=True)[0]
    weight_back = lax.all_gather(expert_out, "rep", axis=1, tiled=True)[0]

    def natural(halves):
        joined = trans_times(pick, jnp.concatenate(halves))
        return joined.astype(jnp.bfloat16)

    packed, *normed_halves = project(tokens_rel, first, second, experts, qkv_width)
    small = natural([half[:, qkv_width - cut :] for half in second])
    gains = small.T.astype(jnp.float32)
    gain_one, gain_two = gains[experts : experts + 1], gains[experts + 1 : experts + 2]
    attended, levels = attention(base, starts, packed, head_size)
    mixed, normed_two, *sending = mix(
        slot_ids_across, tokens, attended, weight_out, gain_two, experts, capacity
    )
    place = me[None].astype(jnp.int32)
    size = capacity // PARTS
    arrived = [trade(after(sending[0], slot_dy))]
    arrived.append(trade(after(sending[1], arrived[0])))
    payloads, kept = [], None
    for part in range(PARTS):
        payload, kept = expert_rows(
            place,
            part,
            arrived[part],
            slot_dy,
            slot_others[:, part * size : (part + 1) * size].reshape(-1, 1),
            small,
            weight_in,
            weight_back,
            kept,
        )
        payloads.append(payload)
    produced, rows_all, slot_grad, active, d_hidden, unused_tails = kept
    payloads[0] = trade(payloads[0])
    payloads[1] = trade(after(payloads[1], payloads[0]))
    rows_all, slot_grad, active, d_hidden = lax.optimization_barrier(
        (rows_all, slot_grad, active, d_hidden, payloads[0])
    )[:4]
    returned = trade(after(produced, payloads[1]))

    in_rows = expert_in.shape[1]
    out_rows = expert_out.shape[1]
    owned_in = scatter_rep(
        lambda who: trans_times(
            lax.dynamic_slice_in_dim(rows_all, who * in_rows, in_rows, 1), d_hidden
        ),
        rep,
    )
    owned_out = scatter_rep(
        lambda who: trans_times(
            lax.dynamic_slice_in_dim(active, who * out_rows, out_rows, 1), slot_grad
        ),
        rep,
    )

    attended_rel = times_trans(attended, pick).astype(jnp.bfloat16)
    normed_rel = times_trans(normed_two, pick).astype(jnp.bfloat16)
    d_mixed, d_attended, gates, *out_pieces = collect(
        slot_ids,
        expert_ids,
        normed_two,
        mixed,
        cotangent,
        small,
        gain_two,
        weight_out,
        pick,
        attended_rel,
        normed_rel,
        payloads,
    )
    d_packed, d_base, *pieces = attention_pull(
        base, starts, packed, d_attended, levels, normed_halves, out_pieces, head_size
    )
    owned, (owned_in, owned_out), mark = ring.scatter(
        *pieces, returned, (owned_in, owned_out)
    )
    weight_qkv = jnp.concatenate(
        [natural(first), natural([half[:, : qkv_width - cut] for half in second])], axis=1
    )
    d_normed_one = times_trans(d_packed, weight_qkv)
    inputs = tokens.astype(jnp.float32)
    unused_one, norm_pull_one = jax.vjp(rms_norm, inputs, gain_one)
    d_inputs_norm, d_gain_one = norm_pull_one(d_normed_one)
    token_grad = d_mixed + d_inputs_norm
    bias_local = jnp.dot(d_base, onehot, precision=highest)
    late = jnp.concatenate([d_gain_one.reshape(-1), bias_local.reshape(-1)])
    late = ring.total(late, returned)
    output = finish(slot_ids, gates, mixed, returned)
    return (
        output,
        token_grad,
        ring.own(late[:model_width]),
        owned[:, :qkv_width],
        owned[:, qkv_width : qkv_width + model_width],
        owned[:, -1],
        owned[:, qkv_width + model_width : qkv_width + model_width + experts],
        add_late(*owned_in, mark)[None],
        add_late(*owned_out, mark)[None],
        late[model_width:].reshape(bias_table.shape),
    )


def solution(mesh):
    return jax.shard_map(
        functools.partial(shards, mesh.shape["fsdp"], mesh.shape["rep"]),
        mesh=mesh,
        in_specs=(
            P(("fsdp", "rep"), None),
            P(("fsdp", "rep")),
            P(("fsdp", "rep"), None),
            P(("fsdp", "rep"), None),
            P(("fsdp", "rep")),
            P(("fsdp", "rep"), None),
            P("fsdp", "rep", None),
            P("fsdp", "rep", None),
            P(),
            P(("fsdp", "rep"), None),
            P(),
            P(("fsdp", "rep"), None),
            P(("fsdp", "rep"), None),
        ),
        out_specs=(
            P(("fsdp", "rep"), None),
            P(("fsdp", "rep"), None),
            P(("fsdp", "rep")),
            P(("fsdp", "rep"), None),
            P(("fsdp", "rep"), None),
            P(("fsdp", "rep")),
            P(("fsdp", "rep"), None),
            P("fsdp", "rep", None),
            P("fsdp", "rep", None),
            P(),
        ),
        check_vma=False,
    )
```
